128 devices in a mesh: dp: 32 (over z, x, core), owner: 4 (over y).
Axes of the slice: x: 4, y: 4, z: 4, core: 2. Of those that a mesh axis runs over, the one named last changes fastest.
Arguments:
- grad: bfloat16 [32, 2048, 4096], P('dp', 'owner'), may hold values from -6 to 6
- error: bfloat16 [32, 2048, 4096], P('dp', 'owner'), may hold values from -4 to 4
- warm_right: float32 [4096, 32], replicated, may hold values from -6 to 6
Outputs:
- update: float32 [2048, 4096], P('owner')
- new_error: float32 [32, 2048, 4096], P('dp', 'owner')
- right_factor: float32 [4096, 32], replicated
The draws below stay inside these ranges and needn't reach their ends.
All inputs are finite; a program needn't handle non-finite values.
Results may differ from the reference program's by a relative error of at most 0.013.
Values may be sent and summed in bfloat16 or wider, within the bound.
No kernel may reach another device: no remote copies, remote signals or barrier semaphores. Data moves between devices by JAX's collectives and lax.ppermute only.
A program may use at most 128 MiB of HBM per device.

```python
import jax
import jax.numpy as jnp
from jax import lax

W = 4096
RANK = 32
ITERS = 4
ROWS = 2048
N_DP = 32


def level_of(own_key, dims, shards, least, largest):
    def one(position, blocks):
        steps = jax.random.uniform(jax.random.fold_in(jax.random.fold_in(own_key, 6), position), (blocks,), jnp.float32, least / len(shards), largest / len(shards))
        return jnp.repeat(jnp.exp(steps), dims[position] // blocks).reshape((-1,) + (1,) * (len(dims) - position - 1))

    gain = one(*shards[0])
    for cut in shards[1:]:
        gain = gain * one(*cut)
    return gain


def scatter_about(key, dims, scale, bound, cuts=(), kind=jnp.bfloat16):
    array = scale * jax.random.normal(key, dims, jnp.float32)
    if cuts:
        array = array * level_of(key, dims, cuts, -0.22, 0.18)
    return jnp.clip(array, -bound, bound).astype(kind)


def setup_inputs(seed: int = 0) -> dict:
    key_list = jax.random.split(jax.random.key(seed), 4)
    grad = scatter_about(key_list[0], (N_DP, ROWS, W), 1.0, 6.0, ((0, 32), (1, 4)))
    error = scatter_about(key_list[1], (N_DP, ROWS, W), 0.5, 4.0, ((0, 32), (1, 4)))
    warm_right = scatter_about(key_list[2], (W, RANK), 1.0, 6.0, (), jnp.float32)
    return {"grad": grad, "error": error, "warm_right": warm_right}


def orthonormal(left):
    gram = jnp.dot(left.T.astype(jnp.float32), left.astype(jnp.float32), precision=lax.Precision.HIGHEST, preferred_element_type=jnp.float32)
    shifted = gram + 1e-06 * (jnp.trace(gram) / RANK) * jnp.eye(RANK, dtype=jnp.float32)
    factor = jnp.linalg.cholesky(shifted)
    solved = jax.scipy.linalg.solve_triangular(factor, left.T, lower=True)
    return solved.T.astype(jnp.bfloat16)

def reference(grad, error, warm_right):
    memory = (grad.astype(jnp.float32) + error.astype(jnp.float32)).astype(jnp.bfloat16)
    right = warm_right
    ortho = jnp.zeros((ROWS, RANK), jnp.bfloat16)
    for step in range(ITERS):
        right_b = right.astype(jnp.bfloat16)

        def add_left(total, block):
            return (total + jnp.dot(block.astype(jnp.float32), right_b.astype(jnp.float32), preferred_element_type=jnp.float32), None)
        left, unused = lax.scan(add_left, jnp.zeros((ROWS, RANK), jnp.float32), memory)
        ortho = orthonormal(left)

        def add_right(total, block):
            return (total + jnp.dot(block.T.astype(jnp.float32), ortho.astype(jnp.float32), preferred_element_type=jnp.float32), None)
        summed, unused = lax.scan(add_right, jnp.zeros((W, RANK), jnp.float32), memory)
        right = summed / N_DP
    update = jnp.dot(ortho.astype(jnp.float32), right.T.astype(jnp.float32), precision=lax.Precision.HIGHEST, preferred_element_type=jnp.float32)
    new_error = memory.astype(jnp.float32) - update[None]
    return (update, new_error, right)
```

```python
import jax
import jax.numpy as jnp
from jax import lax
from jax.experimental import pallas as pl
from jax.experimental.pallas import tpu as pltpu
from jax.sharding import PartitionSpec as P

W = 4096
RANK = 32
ITERS = 4
ROWS = 2048
N_DP = 32
N_OWNER = 4
HALF = W // 2
COLS = HALF // 4
ROWS_OWN = ROWS // N_OWNER
PIECE = ROWS_OWN // 4
MID = ROWS // 2
BF = jnp.bfloat16
F32 = jnp.float32
HIGHEST = lax.Precision.HIGHEST

CORE = [(i, i ^ 1) for i in range(N_DP)]
ZX_GROUPS = [[z * 8 + x * 2 + c for z in range(4) for x in range(4)] for c in range(2)]


def z_shift(k):
    return [(i, i ^ (8 * k)) for i in range(N_DP)]


def xy_groups():
    groups = []
    for z in range(4):
        for c in range(2):
            ys = [(y + 2 * c) % 4 for y in range(4)]
            groups.append([(z * 8 + x * 2 + c) * N_OWNER + y for y in ys for x in range(4)])
    return groups


def params(**kw):
    return pltpu.CompilerParams(vmem_limit_bytes=48 * 1024 * 1024, **kw)


def half_of_memory(grad, error, which):
    def body(which_ref, g_ref, e_ref, o_ref):
        o_ref[...] = (g_ref[...].astype(F32) + e_ref[...].astype(F32)).astype(BF)

    steps = 4
    rows = ROWS_OWN // steps
    spec = pl.BlockSpec((rows, HALF), lambda i, w: (i, w[0]))
    return pl.pallas_call(
        body,
        grid_spec=pltpu.PrefetchScalarGridSpec(
            num_scalar_prefetch=1,
            grid=(steps,),
            in_specs=[spec, spec],
            out_specs=pl.BlockSpec((rows, HALF), lambda i, w: (i, 0)),
        ),
        out_shape=jax.ShapeDtypeStruct((ROWS_OWN, HALF), BF),
        compiler_params=params(),
        name="half_of_memory",
    )(which, grad, error)


def pair_sum(mine, received):
    def body(a_ref, b_ref, o_ref):
        for z in range(4):
            cut = slice(z * COLS, (z + 1) * COLS)
            o_ref[z, 0] = (a_ref[:, cut].astype(F32) + b_ref[:, cut].astype(F32)).astype(BF)

    spec = pl.BlockSpec((PIECE, HALF), lambda x: (x, 0))
    return pl.pallas_call(
        body,
        grid=(4,),
        in_specs=[spec, spec],
        out_specs=pl.BlockSpec((4, 1, PIECE, COLS), lambda x: (0, x, 0, 0)),
        out_shape=jax.ShapeDtypeStruct((4, 4, PIECE, COLS), BF),
        compiler_params=params(),
        name="pair_sum",
    )(mine, received)


def piece_sum(pieces):
    def body(p_ref, o_ref):
        total = p_ref[0].astype(F32)
        for i in range(1, 16):
            total = total + p_ref[i].astype(F32)
        total = total.astype(BF)
        for i in range(16):
            o_ref[i] = total

    rows = 32
    spec = pl.BlockSpec((16, rows, COLS), lambda i: (0, i, 0))
    return pl.pallas_call(
        body,
        grid=(PIECE // rows,),
        in_specs=[spec],
        out_specs=spec,
        out_shape=jax.ShapeDtypeStruct((16, PIECE, COLS), BF),
        compiler_params=params(),
        name="piece_sum",
    )(pieces)


def dot(a, b, dims, precision=None):
    return lax.dot_general(a, b, ((dims[0], dims[1]), ((), ())), precision=precision, preferred_element_type=F32)


def left_from(right_t, m_ref, own_ref, oth_ref):
    left = dot(right_t, m_ref[...], ((1,), (1,)))
    own_ref[...] = left[:, :MID]
    oth_ref[...] = left[:, MID:]


def inverse_factor(gram):
    row = lax.broadcasted_iota(jnp.int32, (RANK, 128), 0)
    lane = lax.broadcasted_iota(jnp.int32, (RANK, 128), 1)
    wide = jnp.concatenate([gram, jnp.zeros((RANK, 128 - RANK), F32)], axis=1)
    trace = jnp.sum(jnp.where(row == lane, wide, 0.0), keepdims=True)
    shift = 1e-06 * (trace / RANK)
    work = wide + jnp.where(row == lane, shift, 0.0) + jnp.where(row + RANK == lane, 1.0, 0.0)
    for k in range(RANK - 1):
        col = jnp.broadcast_to(work[:, k : k + 1], (RANK, 128))
        factor = jnp.where(row > k, col / col[k : k + 1, :], 0.0)
        work = work - factor * work[k : k + 1, :]
    pivot = jnp.sum(jnp.where(row == lane, work, 0.0), axis=1, keepdims=True)
    return work[:, RANK : 2 * RANK] * lax.rsqrt(pivot)


def ortho_from(own_ref, oth_ref):
    left = jnp.concatenate([own_ref[...], oth_ref[...]], axis=1)
    gram = dot(left, left, ((1,), (1,)), HIGHEST)
    return dot(inverse_factor(gram), left, ((1,), (0,)), HIGHEST).astype(BF)


HALVES = (jax.ShapeDtypeStruct((RANK, MID), F32),) * 2


def first_left(right_t, m):
    def body(r_ref, m_ref, own_ref, oth_ref):
        left_from(r_ref[...].astype(BF), m_ref, own_ref, oth_ref)

    return pl.pallas_call(body, out_shape=HALVES, compiler_params=params(), name="first_left")(right_t, m)


def next_left(own, oth, m):
    def body(own_in, oth_in, m_ref, own_ref, oth_ref):
        ortho = ortho_from(own_in, oth_in)
        right = dot(ortho, m_ref[...], ((1,), (0,))) * (1.0 / N_DP)
        left_from(right.astype(BF), m_ref, own_ref, oth_ref)

    return pl.pallas_call(body, out_shape=HALVES, compiler_params=params(), name="next_left")(own, oth, m)


def last_right(own, oth, m):
    def body(own_in, oth_in, m_ref, ortho_ref, right_ref):
        ortho = ortho_from(own_in, oth_in)
        ortho_ref[...] = ortho
        right_ref[...] = dot(ortho, m_ref[...], ((1,), (0,))) * (1.0 / N_DP)

    shapes = (jax.ShapeDtypeStruct((RANK, ROWS), BF), jax.ShapeDtypeStruct((RANK, COLS), F32))
    return pl.pallas_call(body, out_shape=shapes, compiler_params=params(), name="last_right")(own, oth, m)


def sum_over_group(own, oth):
    own = own + lax.ppermute(oth, "dp", CORE)
    a, b, c = [lax.ppermute(own, "dp", z_shift(k)) for k in (1, 3, 2)]
    own = (own + a) + (b + c)
    return own, lax.ppermute(own, "dp", CORE)


def finish(place, ortho, rights, mine, other):
    def body(place_ref, o_ref, r0, r1, r2, r3, mine_ref, other_ref, up_ref, err_ref, right_ref):
        step = pl.program_id(0)
        left = o_ref[...]
        left = jnp.concatenate([left, left, left], axis=0)
        for j in range(2):
            for k, ref in enumerate((r0, r1, r2, r3)):

                @pl.when(step == 4 * j + k)
                def _():
                    right = ref[j * RANK : (j + 1) * RANK, :]
                    right_ref[...] = right
                    high = right.astype(BF)
                    rest = right - high.astype(F32)
                    mid = rest.astype(BF)
                    low = (rest - mid.astype(F32)).astype(BF)
                    update = dot(left, jnp.concatenate([high, mid, low], axis=0), ((0,), (0,)))
                    up_ref[...] = update
                    memory = (mine_ref, other_ref)[j][...].astype(F32)
                    err_ref[...] = memory - update

    def group(s, p):
        return (s % 4) ^ p[0]

    whole = pl.BlockSpec((2 * RANK, COLS), lambda s, p: (0, 0))
    out_block = lambda s, p: (0, ((s // 4) ^ p[1]) * 4 + group(s, p))
    return pl.pallas_call(
        body,
        grid_spec=pltpu.PrefetchScalarGridSpec(
            num_scalar_prefetch=1,
            grid=(8,),
            in_specs=[
                pl.BlockSpec((RANK, ROWS_OWN), lambda s, p: (0, p[2])),
                whole,
                whole,
                whole,
                whole,
                pl.BlockSpec((ROWS_OWN, COLS), lambda s, p: (0, group(jnp.minimum(s, 3), p))),
                pl.BlockSpec((ROWS_OWN, COLS), lambda s, p: (0, group(jnp.maximum(s, 4), p))),
            ],
            out_specs=[
                pl.BlockSpec((ROWS_OWN, COLS), out_block),
                pl.BlockSpec((ROWS_OWN, COLS), out_block),
                pl.BlockSpec((RANK, COLS), out_block),
            ],
        ),
        out_shape=(
            jax.ShapeDtypeStruct((ROWS_OWN, W), F32),
            jax.ShapeDtypeStruct((ROWS_OWN, W), F32),
            jax.ShapeDtypeStruct((RANK, W), F32),
        ),
        compiler_params=params(),
        name="finish",
    )(place, ortho, *rights, mine, other)


def per_device(grad, error, warm_right):
    dp = lax.axis_index("dp")
    owner = lax.axis_index("owner")
    core = dp & 1
    z = dp >> 3

    other = half_of_memory(grad[0], error[0], (1 - core)[None])
    received = lax.ppermute(other, "dp", CORE)
    mine = half_of_memory(grad[0], error[0], core[None])
    blocks = pair_sum(mine, received).reshape(16, PIECE, COLS)
    pieces = lax.all_to_all(blocks, "dp", 0, 0, axis_index_groups=ZX_GROUPS)
    m = lax.all_to_all(piece_sum(pieces), ("dp", "owner"), 0, 0, axis_index_groups=xy_groups())
    m = m.reshape(ROWS, COLS)

    start = core * HALF + z * COLS
    right_t = lax.dynamic_slice(warm_right, (start, 0), (COLS, RANK)).T
    own, oth = first_left(right_t, m)
    for step in range(ITERS - 1):
        own, oth = sum_over_group(own, oth)
        own, oth = next_left(own, oth, m)
    own, oth = sum_over_group(own, oth)
    ortho, right = last_right(own, oth, m)

    pair = jnp.concatenate([right, lax.ppermute(right, "dp", CORE)], axis=0)
    rights = [pair] + [lax.ppermute(pair, "dp", z_shift(k)) for k in (1, 2, 3)]
    row_block = ((owner >> 1) ^ core) * 2 + (owner & 1)
    place = jnp.stack([z, core, row_block]).astype(jnp.int32)
    update, new_error, right_t = finish(place, ortho, rights, mine, other)
    return update, new_error[None], right_t.T


def solution(mesh):
    placed = (P("dp", "owner", None), P("dp", "owner", None), P())
    return jax.shard_map(
        per_device,
        mesh=mesh,
        in_specs=placed,
        out_specs=(P("owner", None), P("dp", "owner", None), P()),
        check_vma=False,
    )
```

```python
import jax
import jax.numpy as jnp
from jax import lax
from jax.experimental import pallas as pl
from jax.experimental.pallas import tpu as pltpu
from jax.sharding import PartitionSpec as P

W = 4096
RANK = 32
ITERS = 4
ROWS = 2048
N_DP = 32
N_OWNER = 4
HALF = W // 2
COLS = HALF // 4
ROWS_OWN = ROWS // N_OWNER
PIECE = ROWS_OWN // 4
MID = ROWS // 2
BF = jnp.bfloat16
F32 = jnp.float32
HIGHEST = lax.Precision.HIGHEST

CORE = [(i, i ^ 1) for i in range(N_DP)]
STEP = {"z": 32, "x": 8, "y": 1}


def along(array, first, second, k):
    step = (STEP[first], STEP[second])
    pairs = [(i, i ^ (k * step[(i >> 2) & 1])) for i in range(N_DP * N_OWNER)]
    return lax.ppermute(array, ("dp", "owner"), pairs)


def exchange(arrays, first, second):
    return [arrays[0]] + [along(arrays[k], first, second, k) for k in (1, 2, 3)]


def spread(array, first, second):
    return exchange([array] * 4, first, second)


def params(**kw):
    return pltpu.CompilerParams(vmem_limit_bytes=48 * 1024 * 1024, **kw)


def half_of_memory(grad, error, which):
    def body(which_ref, g_ref, e_ref, o_ref):
        o_ref[...] = (g_ref[...].astype(F32) + e_ref[...].astype(F32)).astype(BF)

    steps = 4
    rows = ROWS_OWN // steps
    spec = pl.BlockSpec((rows, HALF), lambda i, w: (i, w[0]))
    return pl.pallas_call(
        body,
        grid_spec=pltpu.PrefetchScalarGridSpec(
            num_scalar_prefetch=1,
            grid=(steps,),
            in_specs=[spec, spec],
            out_specs=pl.BlockSpec((rows, HALF), lambda i, w: (i, 0)),
        ),
        out_shape=jax.ShapeDtypeStruct((ROWS_OWN, HALF), BF),
        compiler_params=params(),
        name="half_of_memory",
    )(which, grad, error)


def pair_sum(place, mine, received):
    def body(place_ref, *refs):
        for k in range(4):
            refs[8 + k][0] = (refs[k][...].astype(F32) + refs[4 + k][...].astype(F32)).astype(BF)

    def index(j, p, k):
        first = p[2] == 0
        return jnp.where(first, j, p[1] ^ k), jnp.where(first, p[0] ^ k, j)

    cuts = [pl.BlockSpec((PIECE, COLS), lambda j, p, k=k: index(j, p, k)) for k in range(4)]
    return pl.pallas_call(
        body,
        grid_spec=pltpu.PrefetchScalarGridSpec(
            num_scalar_prefetch=1,
            grid=(4,),
            in_specs=cuts + cuts,
            out_specs=[pl.BlockSpec((1, PIECE, COLS), lambda j, p: (j, 0, 0))] * 4,
        ),
        out_shape=[jax.ShapeDtypeStruct((4, PIECE, COLS), BF)] * 4,
        compiler_params=params(),
        name="pair_sum",
    )(place, *[mine] * 4, *[received] * 4)


SCALARS = pl.BlockSpec(memory_space=pltpu.SMEM)
WHOLE = pl.BlockSpec(memory_space=pltpu.VMEM)


def call(body, name, out_shape, place, *arrays):
    return pl.pallas_call(
        body,
        in_specs=[SCALARS] + [WHOLE] * len(arrays),
        out_specs=jax.tree.map(lambda s: WHOLE, out_shape),
        out_shape=out_shape,
        compiler_params=params(),
        name=name,
    )(place, *arrays)


def cut(index, size):
    return pl.ds(pl.multiple_of(index * size, size), size)


def first_sum(place, parts):
    def body(place_ref, *refs):
        own = jnp.where(place_ref[2] == 0, place_ref[1], place_ref[0])
        for k in range(4):
            total = refs[0][own ^ k].astype(F32)
            for ref in refs[1:4]:
                total = total + ref[own ^ k].astype(F32)
            refs[4 + k][...] = total.astype(BF)

    return call(body, "first_sum", [jax.ShapeDtypeStruct((PIECE, COLS), BF)] * 4, place, *parts)


def second_sum(place, parts):
    def body(place_ref, a_ref, b_ref, c_ref, d_ref, o_ref):
        total = a_ref[...].astype(F32) + b_ref[...].astype(F32)
        o_ref[...] = (total + (c_ref[...].astype(F32) + d_ref[...].astype(F32))).astype(BF)

    return call(body, "second_sum", jax.ShapeDtypeStruct((PIECE, COLS), BF), place, *parts)


def thirds(x):
    high = x.astype(BF)
    rest = x - high.astype(F32)
    mid = rest.astype(BF)
    low = (rest - mid.astype(F32)).astype(BF)
    return jnp.concatenate([high, mid, low], axis=0)


def dot(a, b, dims, precision=None):
    return lax.dot_general(a, b, ((dims[0], dims[1]), ((), ())), precision=precision, preferred_element_type=F32)


def thirds(x):
    high = x.astype(BF)
    rest = x - high.astype(F32)
    mid = rest.astype(BF)
    low = (rest - mid.astype(F32)).astype(BF)
    return jnp.concatenate([high, mid, low], axis=0)


def add_thirds(x):
    return x[:RANK] + (x[RANK : 2 * RANK] + x[2 * RANK :])


def reorder(rows, place_ref):
    blocks = [rows[:, i * PIECE : (i + 1) * PIECE] for i in range(16)]
    swapped = jnp.concatenate([blocks[(i % 4) * 4 + i // 4] for i in range(16)], axis=1)
    return jnp.where(place_ref[2] == 0, rows, swapped)


def store_halves(place_ref, left, own_ref, oth_ref):
    left = reorder(left, place_ref)
    low, high = left[:, :MID], left[:, MID:]
    first = place_ref[2] == 0
    own_ref[...] = jnp.where(first, low, high)
    oth_ref[...] = jnp.where(first, high, low)


def load_halves(place_ref, own_ref, oth_ref):
    first = place_ref[2] == 0
    own, oth = own_ref[...], oth_ref[...]
    return jnp.concatenate([jnp.where(first, own, oth), jnp.where(first, oth, own)], axis=1)


def times_m(rows, m_refs):
    parts = [dot(rows[:, i * ROWS_OWN : (i + 1) * ROWS_OWN], ref[...], ((1,), (0,))) for i, ref in enumerate(m_refs)]
    return (parts[0] + parts[1]) + (parts[2] + parts[3])


def times_m_t(rows, m_refs):
    return jnp.concatenate([dot(rows, ref[...], ((1,), (1,))) for ref in m_refs], axis=1)


def inverse_factor(gram):
    row = lax.broadcasted_iota(jnp.int32, (RANK, 128), 0)
    lane = lax.broadcasted_iota(jnp.int32, (RANK, 128), 1)
    wide = jnp.concatenate([gram, jnp.zeros((RANK, 128 - RANK), F32)], axis=1)
    trace = jnp.sum(jnp.where(row == lane, wide, 0.0), keepdims=True)
    shift = 1e-06 * (trace / RANK)
    work = wide + jnp.where(row == lane, shift, 0.0) + jnp.where(row + RANK == lane, 1.0, 0.0)
    for k in range(RANK - 1):
        col = jnp.broadcast_to(work[:, k : k + 1], (RANK, 128))
        factor = jnp.where(row > k, col / col[k : k + 1, :], 0.0)
        work = work - factor * work[k : k + 1, :]
    pivot = jnp.sum(jnp.where(row == lane, work, 0.0), axis=1, keepdims=True)
    return work[:, RANK : 2 * RANK] * lax.rsqrt(pivot)


HALVES = [jax.ShapeDtypeStruct((RANK, MID), F32)] * 2


def first_left(place, right_t, m):
    def body(place_ref, r_ref, m0, m1, m2, m3, own_ref, oth_ref):
        cols = cut(place_ref[2] * 4 + place_ref[0], COLS)
        left = times_m_t(r_ref[:, cols].astype(BF), (m0, m1, m2, m3))
        store_halves(place_ref, left, own_ref, oth_ref)

    return call(body, "first_left", HALVES, place, right_t, *m)


def next_left(place, own, oth, inverse, m):
    def body(place_ref, own_in, oth_in, *refs):
        left = load_halves(place_ref, own_in, oth_in)
        if inverse is not None:
            left = dot(refs[0][...], left, ((1,), (0,)), HIGHEST) * (1.0 / N_DP)
            refs = refs[1:]
        m_refs, (left_ref, own_ref, oth_ref) = refs[:4], refs[4:]
        left_ref[...] = left
        right = add_thirds(times_m(thirds(reorder(left, place_ref)), m_refs))
        following = add_thirds(times_m_t(thirds(right), m_refs))
        store_halves(place_ref, following, own_ref, oth_ref)

    shapes = [jax.ShapeDtypeStruct((RANK, ROWS), F32)] + HALVES
    extra = [] if inverse is None else [inverse]
    return call(body, "next_left", shapes, place, own, oth, *extra, *m)


def inverse_of(place, left):
    def body(place_ref, left_ref, o_ref):
        left = left_ref[...]
        o_ref[...] = inverse_factor(dot(left, left, ((1,), (1,)), HIGHEST))

    return call(body, "inverse_of", jax.ShapeDtypeStruct((RANK, RANK), F32), place, left)


def last_right(place, own, oth, inverse, m):
    def body(place_ref, own_in, oth_in, inv_ref, m0, m1, m2, m3, ortho_ref, right_ref):
        left = load_halves(place_ref, own_in, oth_in)
        left = dot(inv_ref[...], left, ((1,), (0,)), HIGHEST) * (1.0 / N_DP)
        gram = dot(left, left, ((1,), (1,)), HIGHEST)
        ortho = dot(inverse_factor(gram), left, ((1,), (0,)), HIGHEST).astype(BF)
        for k in range(4):
            ortho_ref[:, cut(place_ref[1] ^ k, PIECE)] = ortho[:, k * PIECE : (k + 1) * PIECE]
        right_ref[...] = times_m(reorder(ortho, place_ref), (m0, m1, m2, m3)) * (1.0 / N_DP)

    shapes = [jax.ShapeDtypeStruct((RANK, ROWS_OWN), BF), jax.ShapeDtypeStruct((RANK, COLS), F32)]
    return call(body, "last_right", shapes, place, own, oth, inverse, *m)


def sum_over_group(own, oth, beside=None):
    own = own + lax.ppermute(oth, "dp", CORE)
    parts = spread(own, "z", "z")
    if beside is not None:
        parts, beside = lax.optimization_barrier((parts, beside))
    a, b, c, d = parts
    own = (a + b) + (c + d)
    return own, lax.ppermute(own, "dp", CORE), beside


def finish(place, ortho, rights, mine, other):
    def body(place_ref, o_ref, r0, r1, r2, r3, mine_ref, other_ref, up_ref, err_ref, right_ref):
        step = pl.program_id(0)
        left = jnp.concatenate([o_ref[...]] * 3, axis=0)
        for j in range(2):
            for k, ref in enumerate((r0, r1, r2, r3)):

                @pl.when(step == 4 * j + k)
                def _():
                    right = ref[j * RANK : (j + 1) * RANK, :]
                    right_ref[...] = right
                    update = dot(left, thirds(right), ((0,), (0,)))
                    up_ref[...] = update
                    memory = (mine_ref, other_ref)[j][...].astype(F32)
                    err_ref[...] = memory - update

    def group(s, p):
        return (s % 4) ^ p[0]

    whole = pl.BlockSpec((2 * RANK, COLS), lambda s, p: (0, 0))
    out_block = lambda s, p: (0, ((s // 4) ^ p[2]) * 4 + group(s, p))
    return pl.pallas_call(
        body,
        grid_spec=pltpu.PrefetchScalarGridSpec(
            num_scalar_prefetch=1,
            grid=(8,),
            in_specs=[
                pl.BlockSpec((RANK, ROWS_OWN), lambda s, p: (0, 0)),
                whole,
                whole,
                whole,
                whole,
                pl.BlockSpec((ROWS_OWN, COLS), lambda s, p: (0, group(jnp.minimum(s, 3), p))),
                pl.BlockSpec((ROWS_OWN, COLS), lambda s, p: (0, group(jnp.maximum(s, 4), p))),
            ],
            out_specs=[
                pl.BlockSpec((ROWS_OWN, COLS), out_block),
                pl.BlockSpec((ROWS_OWN, COLS), out_block),
                pl.BlockSpec((RANK, COLS), out_block),
            ],
        ),
        out_shape=(
            jax.ShapeDtypeStruct((ROWS_OWN, W), F32),
            jax.ShapeDtypeStruct((ROWS_OWN, W), F32),
            jax.ShapeDtypeStruct((RANK, W), F32),
        ),
        compiler_params=params(),
        name="finish",
    )(place, ortho, *rights, mine, other)


def per_device(grad, error, warm_right):
    dp = lax.axis_index("dp")
    core = dp & 1
    place = jnp.stack([dp >> 3, (dp >> 1) & 3, core]).astype(jnp.int32)

    other = half_of_memory(grad[0], error[0], (1 - core)[None])
    received = lax.ppermute(other, "dp", CORE)
    mine = half_of_memory(grad[0], error[0], core[None])
    pairs = exchange(pair_sum(place, mine, received), "z", "x")
    piece = second_sum(place, exchange(first_sum(place, pairs), "x", "z"))
    m = spread(jnp.concatenate(spread(piece, "x", "y"), axis=0), "y", "x")

    own, oth, inverse = sum_over_group(*first_left(place, warm_right.T, m))
    for step in range(ITERS - 1):
        left, own, oth = next_left(place, own, oth, inverse, m)
        own, oth, inverse = sum_over_group(own, oth, inverse_of(place, left))
    ortho, right = last_right(place, own, oth, inverse, m)

    pair = jnp.concatenate([right, lax.ppermute(right, "dp", CORE)], axis=0)
    update, new_error, right_t = finish(place, ortho, spread(pair, "z", "z"), mine, other)
    return update, new_error[None], right_t.T


def solution(mesh):
    placed = (P("dp", "owner", None), P("dp", "owner", None), P())
    return jax.shard_map(
        per_device,
        mesh=mesh,
        in_specs=placed,
        out_specs=(P("owner", None), P("dp", "owner", None), P()),
        check_vma=False,
    )
```

```python
import jax
import jax.numpy as jnp
from jax import lax
from jax.experimental import pallas as pl
from jax.experimental.pallas import tpu as pltpu
from jax.sharding import PartitionSpec as P

W = 4096
RANK = 32
ITERS = 4
ROWS = 2048
N_DP = 32
N_OWNER = 4
HALF = W // 2
COLS = HALF // 4
ROWS_OWN = ROWS // N_OWNER
PIECE = ROWS_OWN // 4
MID = ROWS // 2
PANEL = 8
BF = jnp.bfloat16
F32 = jnp.float32
HIGHEST = lax.Precision.HIGHEST

CORE = [(i, i ^ 1) for i in range(N_DP)]
STEP = {"z": 32, "x": 8, "y": 1}


def along(array, first, second, k):
    step = (STEP[first], STEP[second])
    pairs = [(i, i ^ (k * step[(i >> 2) & 1])) for i in range(N_DP * N_OWNER)]
    return lax.ppermute(array, ("dp", "owner"), pairs)


def exchange(arrays, first, second):
    return [arrays[0]] + [along(arrays[k], first, second, k) for k in (1, 2, 3)]


def spread(array, first, second):
    return exchange([array] * 4, first, second)


def params(**kw):
    return pltpu.CompilerParams(vmem_limit_bytes=48 * 1024 * 1024, **kw)


SCALARS = pl.BlockSpec(memory_space=pltpu.SMEM)
WHOLE = pl.BlockSpec(memory_space=pltpu.VMEM)
HBM = pl.BlockSpec(memory_space=pl.ANY)


def half_of_memory(grad, error, which):
    chunks = 8
    rows = ROWS_OWN // chunks

    def body(which_ref, g_hbm, e_hbm, o_ref, g_ref, e_ref, sems):
        cols = cut(which_ref[0], HALF)
        copies = []
        for i in range(chunks):
            part = pl.ds(i * rows, rows)
            pair = [
                pltpu.make_async_copy(src.at[part, cols], dst.at[part, :], sems.at[n, i])
                for n, (src, dst) in enumerate(((g_hbm, g_ref), (e_hbm, e_ref)))
            ]
            for copy in pair:
                copy.start()
            copies.append(pair)
        for i, pair in enumerate(copies):
            for copy in pair:
                copy.wait()
            part = pl.ds(i * rows, rows)
            o_ref[part, :] = (g_ref[part, :].astype(F32) + e_ref[part, :].astype(F32)).astype(BF)

    return pl.pallas_call(
        body,
        in_specs=[SCALARS, HBM, HBM],
        out_specs=WHOLE,
        scratch_shapes=[pltpu.VMEM((ROWS_OWN, HALF), BF)] * 2 + [pltpu.SemaphoreType.DMA((2, chunks))],
        out_shape=jax.ShapeDtypeStruct((ROWS_OWN, HALF), BF),
        compiler_params=params(),
        name="half_of_memory",
    )(which, grad, error)


def call(body, name, out_shape, place, *arrays, scratch=()):
    return pl.pallas_call(
        body,
        in_specs=[SCALARS] + [WHOLE] * len(arrays),
        out_specs=jax.tree.map(lambda s: WHOLE, out_shape),
        out_shape=out_shape,
        scratch_shapes=scratch,
        compiler_params=params(),
        name=name,
    )(place, *arrays)


def cut(index, size):
    return pl.ds(pl.multiple_of(index * size, size), size)


def pair_sum(place, mine, received):
    def body(place_ref, a_ref, b_ref, *out):
        first = place_ref[2] == 0
        for k in range(4):
            for j in range(4):
                rows = cut(jnp.where(first, j, place_ref[1] ^ k), PIECE)
                cols = cut(jnp.where(first, place_ref[0] ^ k, j), COLS)
                out[k][j] = a_ref[rows, cols] + b_ref[rows, cols]

    return call(body, "pair_sum", [jax.ShapeDtypeStruct((4, PIECE, COLS), BF)] * 4, place, mine, received)


def first_sum(place, parts):
    def body(place_ref, *refs):
        own = jnp.where(place_ref[2] == 0, place_ref[1], place_ref[0])
        for k in range(4):
            total = refs[0][own ^ k].astype(F32)
            for ref in refs[1:4]:
                total = total + ref[own ^ k].astype(F32)
            refs[4 + k][...] = total.astype(BF)

    return call(body, "first_sum", [jax.ShapeDtypeStruct((PIECE, COLS), BF)] * 4, place, *parts)


def second_sum(place, parts):
    def body(place_ref, a_ref, b_ref, c_ref, d_ref, o_ref):
        total = a_ref[...].astype(F32) + b_ref[...].astype(F32)
        o_ref[...] = (total + (c_ref[...].astype(F32) + d_ref[...].astype(F32))).astype(BF)

    return call(body, "second_sum", jax.ShapeDtypeStruct((PIECE, COLS), BF), place, *parts)


def early_left(place, warm_t, pairs):
    def body(place_ref, warm_ref, *refs):
        pairs, (own_ref, oth_ref, sum_ref) = refs[:4], refs[4:]
        core = place_ref[2]
        sum_ref[...] = jnp.zeros((RANK, ROWS_OWN), F32)
        for k in range(4):
            for j in range(4):
                rows = cut(jnp.where(core == 0, j, place_ref[1] ^ k), PIECE)
                group = jnp.where(core == 0, place_ref[0] ^ k, j)
                right = warm_ref[:, cut(core * 4 + group, COLS)].astype(BF)
                sum_ref[:, rows] += dot(right, pairs[k][j], ((1,), (1,)))
        own_ref[...] = sum_ref[:, cut(core, ROWS_OWN // 2)]
        oth_ref[...] = sum_ref[:, cut(1 - core, ROWS_OWN // 2)]

    shapes = [jax.ShapeDtypeStruct((RANK, ROWS_OWN // 2), F32)] * 2
    scratch = [pltpu.VMEM((RANK, ROWS_OWN), F32)]
    return call(body, "early_left", shapes, place, warm_t, *pairs, scratch=scratch)


def assemble_left(place, own, oth):
    def body(place_ref, own_ref, oth_ref, o_ref, sum_ref):
        core, half = place_ref[2], ROWS_OWN // 2
        for y in range(4):
            rows = slice(y * RANK, (y + 1) * RANK)
            sum_ref[:, cut(2 * y + core, half)] = own_ref[rows, :]
            sum_ref[:, cut(2 * y + 1 - core, half)] = oth_ref[rows, :]
        for y in range(4):
            for x in range(4):
                i = 4 * y + x
                o_ref[:, i * PIECE : (i + 1) * PIECE] = sum_ref[:, cut(4 * y + (place_ref[1] ^ x), PIECE)]

    shape = jax.ShapeDtypeStruct((RANK, ROWS), F32)
    return call(body, "assemble_left", shape, place, own, oth, scratch=[pltpu.VMEM((RANK, ROWS), F32)])


def thirds(x):
    high = x.astype(BF)
    rest = x - high.astype(F32)
    mid = rest.astype(BF)
    low = (rest - mid.astype(F32)).astype(BF)
    return jnp.concatenate([high, mid, low], axis=0)


def dot(a, b, dims, precision=None):
    return lax.dot_general(a, b, ((dims[0], dims[1]), ((), ())), precision=precision, preferred_element_type=F32)


def thirds(x):
    high = x.astype(BF)
    rest = x - high.astype(F32)
    mid = rest.astype(BF)
    low = (rest - mid.astype(F32)).astype(BF)
    return jnp.concatenate([high, mid, low], axis=0)


def add_thirds(x):
    return x[:RANK] + (x[RANK : 2 * RANK] + x[2 * RANK :])


def reorder(rows, place_ref):
    blocks = [rows[:, i * PIECE : (i + 1) * PIECE] for i in range(16)]
    swapped = jnp.concatenate([blocks[(i % 4) * 4 + i // 4] for i in range(16)], axis=1)
    return jnp.where(place_ref[2] == 0, rows, swapped)


def store_halves(place_ref, left, own_ref, oth_ref):
    left = reorder(left, place_ref)
    low, high = left[:, :MID], left[:, MID:]
    first = place_ref[2] == 0
    own_ref[...] = jnp.where(first, low, high)
    oth_ref[...] = jnp.where(first, high, low)


def load_halves(place_ref, own_ref, oth_ref):
    first = place_ref[2] == 0
    own, oth = own_ref[...], oth_ref[...]
    return jnp.concatenate([jnp.where(first, own, oth), jnp.where(first, oth, own)], axis=1)


def times_m(rows, m_refs):
    parts = [dot(rows[:, i * ROWS_OWN : (i + 1) * ROWS_OWN], ref[...], ((1,), (0,))) for i, ref in enumerate(m_refs)]
    return (parts[0] + parts[1]) + (parts[2] + parts[3])


def times_m_t(rows, m_refs):
    return jnp.concatenate([dot(rows, ref[...], ((1,), (1,))) for ref in m_refs], axis=1)


def inverse_factor(gram):
    row = lax.broadcasted_iota(jnp.int32, (RANK, 128), 0)
    lane = lax.broadcasted_iota(jnp.int32, (RANK, 128), 1)
    wide = jnp.concatenate([gram, jnp.zeros((RANK, 128 - RANK), F32)], axis=1)
    trace = jnp.sum(jnp.where(row == lane, wide, 0.0), keepdims=True)
    shift = 1e-06 * (trace / RANK)
    work = wide + jnp.where(row == lane, shift, 0.0) + jnp.where(row + RANK == lane, 1.0, 0.0)
    for start in range(0, RANK, PANEL):
        cols = [jnp.broadcast_to(work[:, start + j : start + j + 1], (RANK, 128)) for j in range(PANEL)]
        for j in range(PANEL):
            k = start + j
            factor = jnp.where(row > k, cols[j] * (1.0 / cols[j][k : k + 1, :]), 0.0)
            work = work - factor * work[k : k + 1, :]
            for i in range(j + 1, PANEL):
                cols[i] = cols[i] - factor * cols[i][k : k + 1, :]
    pivot = jnp.sum(jnp.where(row == lane, work, 0.0), axis=1, keepdims=True)
    return work[:, RANK : 2 * RANK] * lax.rsqrt(pivot)


HALVES = [jax.ShapeDtypeStruct((RANK, MID), F32)] * 2


def second_left(place, left, inverse, m):
    def body(place_ref, left_ref, inv_ref, *refs):
        m_refs, (own_ref, oth_ref) = refs[:4], refs[4:]
        ortho = dot(inv_ref[...], left_ref[...], ((1,), (0,)), HIGHEST).astype(BF)
        right = times_m(reorder(ortho, place_ref), m_refs) * (1.0 / N_DP)
        store_halves(place_ref, times_m_t(right.astype(BF), m_refs), own_ref, oth_ref)

    return call(body, "second_left", HALVES, place, left, inverse, *m)


def next_left(place, own, oth, inverse, m):
    def body(place_ref, own_in, oth_in, *refs):
        left = load_halves(place_ref, own_in, oth_in)
        if inverse is not None:
            left = dot(refs[0][...], left, ((1,), (0,)), HIGHEST) * (1.0 / N_DP)
            refs = refs[1:]
        m_refs, (left_ref, own_ref, oth_ref) = refs[:4], refs[4:]
        left_ref[...] = left
        right = add_thirds(times_m(thirds(reorder(left, place_ref)), m_refs))
        following = add_thirds(times_m_t(thirds(right), m_refs))
        store_halves(place_ref, following, own_ref, oth_ref)

    shapes = [jax.ShapeDtypeStruct((RANK, ROWS), F32)] + HALVES
    extra = [] if inverse is None else [inverse]
    return call(body, "next_left", shapes, place, own, oth, *extra, *m)


def inverse_of(place, left):
    def body(place_ref, left_ref, o_ref):
        left = left_ref[...]
        o_ref[...] = inverse_factor(dot(left, left, ((1,), (1,)), HIGHEST))

    return call(body, "inverse_of", jax.ShapeDtypeStruct((RANK, RANK), F32), place, left)


def last_right(place, own, oth, inverse, m):
    def body(place_ref, own_in, oth_in, inv_ref, m0, m1, m2, m3, ortho_ref, right_ref):
        left = load_halves(place_ref, own_in, oth_in)
        left = dot(inv_ref[...], left, ((1,), (0,)), HIGHEST) * (1.0 / N_DP)
        gram = dot(left, left, ((1,), (1,)), HIGHEST)
        ortho = dot(inverse_factor(gram), left, ((1,), (0,)), HIGHEST).astype(BF)
        for k in range(4):
            ortho_ref[:, cut(place_ref[1] ^ k, PIECE)] = ortho[:, k * PIECE : (k + 1) * PIECE]
        right_ref[...] = times_m(reorder(ortho, place_ref), (m0, m1, m2, m3)) * (1.0 / N_DP)

    shapes = [jax.ShapeDtypeStruct((RANK, ROWS_OWN), BF), jax.ShapeDtypeStruct((RANK, COLS), F32)]
    return call(body, "last_right", shapes, place, own, oth, inverse, *m)


def sum_over_group(own, oth, beside=None):
    own = own + lax.ppermute(oth, "dp", CORE)
    parts = spread(own, "z", "z")
    if beside is not None:
        parts, beside = lax.optimization_barrier((parts, beside))
    a, b, c, d = parts
    own = (a + b) + (c + d)
    return own, lax.ppermute(own, "dp", CORE), beside


def columns_of(place, ortho):
    def body(place_ref, o_ref, out_ref):
        wide = jnp.concatenate([o_ref[...].astype(F32)] * 3 + [jnp.zeros((RANK, ROWS_OWN), F32)], axis=0)
        out_ref[...] = wide.T.astype(BF)

    return call(body, "columns_of", jax.ShapeDtypeStruct((ROWS_OWN, 4 * RANK), BF), place, ortho)


def finish(place, ortho, rights, mine, other, outs, name):
    keys = list(rights)
    count, kept = len(keys), len(outs)

    def body(place_ref, o_ref, *refs):
        rights, memory, refs = refs[:count], refs[count : count + 2], refs[count + 2 + kept :]
        up_hbm, err_hbm, right_hbm, up_ref, err_ref, sems = refs
        copies = []

        def send(i, n, source, target):
            copies.append(pltpu.make_async_copy(source, target, sems.at[i, n]))
            copies[-1].start()

        for n, ((k, j), ref) in enumerate(zip(keys, rights)):
            z = place_ref[0] ^ k
            cols = cut((place_ref[2] ^ j) * 4 + z, COLS)
            wide = jnp.concatenate([thirds(ref[...]), jnp.zeros((RANK, COLS), BF)], axis=0)
            update = dot(o_ref[...], wide, ((1,), (0,)))
            up_ref[n] = update
            send(0, n, up_ref.at[n], up_hbm.at[:, cols])
            err_ref[n] = memory[j][:, cut(z, COLS)].astype(F32) - update
            send(1, n, err_ref.at[n], err_hbm.at[:, cols])
            send(2, n, ref, right_hbm.at[:, cols])
        for copy in copies:
            copy.wait()

    blocks = pltpu.VMEM((count, ROWS_OWN, COLS), F32)
    return pl.pallas_call(
        body,
        in_specs=[SCALARS] + [WHOLE] * (count + 3) + [HBM] * kept,
        out_specs=[HBM] * 3,
        scratch_shapes=[blocks, blocks, pltpu.SemaphoreType.DMA((3, count))],
        out_shape=(
            jax.ShapeDtypeStruct((ROWS_OWN, W), F32),
            jax.ShapeDtypeStruct((ROWS_OWN, W), F32),
            jax.ShapeDtypeStruct((RANK, W), F32),
        ),
        input_output_aliases={count + 4 + i: i for i in range(kept)},
        compiler_params=params(),
        name=name,
    )(place, ortho, *rights.values(), mine, other, *outs)


def per_device(grad, error, warm_right):
    dp = lax.axis_index("dp")
    core = dp & 1
    place = jnp.stack([dp >> 3, (dp >> 1) & 3, core]).astype(jnp.int32)

    other = half_of_memory(grad[0], error[0], (1 - core)[None])
    received = lax.ppermute(other, "dp", CORE)
    mine = half_of_memory(grad[0], error[0], core[None])
    pairs = pair_sum(place, mine, received)
    early, passed = early_left(place, warm_right.T, pairs)
    early = early + lax.ppermute(passed, "dp", CORE)
    parts, early = lax.optimization_barrier((exchange(pairs, "z", "x"), spread(early, "x", "x")))
    early = (early[0] + early[1]) + (early[2] + early[3])
    parts = exchange(first_sum(place, parts), "x", "z")
    parts, early = lax.optimization_barrier((parts, spread(early, "y", "y")))
    m, early = lax.optimization_barrier((spread(second_sum(place, parts), "x", "y"), early))
    early = spread(jnp.concatenate(early, axis=0), "z", "z")
    early = (early[0] + early[1]) + (early[2] + early[3])
    left = assemble_left(place, early, lax.ppermute(early, "dp", CORE))
    m = spread(jnp.concatenate(m, axis=0), "y", "x")
    m, left, inverse = lax.optimization_barrier((m, left, inverse_of(place, left)))

    own, oth, inverse = sum_over_group(*second_left(place, left, inverse, m))
    for step in range(ITERS - 2):
        left, own, oth = next_left(place, own, oth, inverse, m)
        own, oth, inverse = sum_over_group(own, oth, inverse_of(place, left))
    ortho, right = last_right(place, own, oth, inverse, m)

    ortho = columns_of(place, ortho)
    near = {(0, 0): right, (0, 1): lax.ppermute(right, "dp", CORE)}
    outs = finish(place, ortho, near, mine, other, [], "finish_near")
    rights, outs = lax.optimization_barrier((spread(right, "z", "z"), outs))
    far = {(k, 0): rights[k] for k in (1, 2, 3)}
    far.update({(k, 1): lax.ppermute(rights[k], "dp", CORE) for k in (1, 2, 3)})
    update, new_error, right_t = finish(place, ortho, far, mine, other, outs, "finish_far")
    return update, new_error[None], right_t.T


def solution(mesh):
    placed = (P("dp", "owner", None), P("dp", "owner", None), P())
    return jax.shard_map(
        per_device,
        mesh=mesh,
        in_specs=placed,
        out_specs=(P("owner", None), P("dp", "owner", None), P()),
        check_vma=False,
    )
```

```python
import jax
import jax.numpy as jnp
from jax import lax
from jax.experimental import pallas as pl
from jax.experimental.pallas import tpu as pltpu
from jax.sharding import PartitionSpec as P

W = 4096
RANK = 32
ITERS = 4
ROWS = 2048
N_DP = 32
N_OWNER = 4
HALF = W // 2
COLS = HALF // 4
ROWS_OWN = ROWS // N_OWNER
PIECE = ROWS_OWN // 4
MID = ROWS // 2
PANEL = 8
BF = jnp.bfloat16
F32 = jnp.float32
HIGHEST = lax.Precision.HIGHEST

CORE = [(i, i ^ 1) for i in range(N_DP)]
STEP = {"z": 32, "x": 8, "y": 1}


def along(array, first, second, k):
    step = (STEP[first], STEP[second])
    pairs = [(i, i ^ (k * step[(i >> 2) & 1])) for i in range(N_DP * N_OWNER)]
    return lax.ppermute(array, ("dp", "owner"), pairs)


def exchange(arrays, first, second):
    return [arrays[0]] + [along(arrays[k], first, second, k) for k in (1, 2, 3)]


def spread(array, first, second):
    return exchange([array] * 4, first, second)


def params(**kw):
    return pltpu.CompilerParams(vmem_limit_bytes=48 * 1024 * 1024, **kw)


SCALARS = pl.BlockSpec(memory_space=pltpu.SMEM)
WHOLE = pl.BlockSpec(memory_space=pltpu.VMEM)
HBM = pl.BlockSpec(memory_space=pl.ANY)
SMALL = pl.CostEstimate(flops=1000, bytes_accessed=1000, transcendentals=0)


def half_of_memory(grad, error, which):
    chunks = 8
    rows = ROWS_OWN // chunks

    def body(which_ref, g_hbm, e_hbm, o_ref, g_ref, e_ref, sems):
        cols = cut(which_ref[0], HALF)
        copies = []
        for i in range(chunks):
            part = pl.ds(i * rows, rows)
            pair = [
                pltpu.make_async_copy(src.at[part, cols], dst.at[part, :], sems.at[n, i])
                for n, (src, dst) in enumerate(((g_hbm, g_ref), (e_hbm, e_ref)))
            ]
            for copy in pair:
                copy.start()
            copies.append(pair)
        for i, pair in enumerate(copies):
            for copy in pair:
                copy.wait()
            part = pl.ds(i * rows, rows)
            o_ref[part, :] = (g_ref[part, :].astype(F32) + e_ref[part, :].astype(F32)).astype(BF)

    return pl.pallas_call(
        body,
        in_specs=[SCALARS, HBM, HBM],
        out_specs=WHOLE,
        scratch_shapes=[pltpu.VMEM((ROWS_OWN, HALF), BF)] * 2 + [pltpu.SemaphoreType.DMA((2, chunks))],
        out_shape=jax.ShapeDtypeStruct((ROWS_OWN, HALF), BF),
        compiler_params=params(),
        name="half_of_memory",
    )(which, grad, error)


def call(body, name, out_shape, place, *arrays, scratch=(), cost=None):
    return pl.pallas_call(
        body,
        in_specs=[SCALARS] + [WHOLE] * len(arrays),
        out_specs=jax.tree.map(lambda s: WHOLE, out_shape),
        out_shape=out_shape,
        scratch_shapes=scratch,
        cost_estimate=cost,
        compiler_params=params(),
        name=name,
    )(place, *arrays)


def cut(index, size):
    return pl.ds(pl.multiple_of(index * size, size), size)


def pair_sum(place, mine, received):
    def body(place_ref, a_ref, b_ref, *out):
        first = place_ref[2] == 0
        for k in range(4):
            for j in range(4):
                rows = cut(jnp.where(first, j, place_ref[1] ^ k), PIECE)
                cols = cut(jnp.where(first, place_ref[0] ^ k, j), COLS)
                out[k][j] = a_ref[rows, cols] + b_ref[rows, cols]

    return call(body, "pair_sum", [jax.ShapeDtypeStruct((4, PIECE, COLS), BF)] * 4, place, mine, received)


def first_sum(place, parts):
    def body(place_ref, *refs):
        own = jnp.where(place_ref[2] == 0, place_ref[1], place_ref[0])
        for k in range(4):
            total = refs[0][own ^ k].astype(F32)
            for ref in refs[1:4]:
                total = total + ref[own ^ k].astype(F32)
            refs[4 + k][...] = total.astype(BF)

    return call(body, "first_sum", [jax.ShapeDtypeStruct((PIECE, COLS), BF)] * 4, place, *parts)


def second_sum(place, parts):
    def body(place_ref, a_ref, b_ref, c_ref, d_ref, o_ref):
        total = a_ref[...].astype(F32) + b_ref[...].astype(F32)
        o_ref[...] = (total + (c_ref[...].astype(F32) + d_ref[...].astype(F32))).astype(BF)

    return call(body, "second_sum", jax.ShapeDtypeStruct((PIECE, COLS), BF), place, *parts)


def early_left(place, warm_t, pairs):
    def body(place_ref, warm_ref, *refs):
        pairs, (own_ref, oth_ref, sum_ref) = refs[:4], refs[4:]
        core = place_ref[2]
        sum_ref[...] = jnp.zeros((RANK, ROWS_OWN), F32)
        for k in range(4):
            for j in range(4):
                rows = cut(jnp.where(core == 0, j, place_ref[1] ^ k), PIECE)
                group = jnp.where(core == 0, place_ref[0] ^ k, j)
                right = warm_ref[:, cut(core * 4 + group, COLS)].astype(BF)
                sum_ref[:, rows] += dot(right, pairs[k][j], ((1,), (1,)))
        own_ref[...] = sum_ref[:, cut(core, ROWS_OWN // 2)]
        oth_ref[...] = sum_ref[:, cut(1 - core, ROWS_OWN // 2)]

    shapes = [jax.ShapeDtypeStruct((RANK, ROWS_OWN // 2), F32)] * 2
    scratch = [pltpu.VMEM((RANK, ROWS_OWN), F32)]
    return call(body, "early_left", shapes, place, warm_t, *pairs, scratch=scratch)


def stack_early(place, parts, after):
    def body(place_ref, a_ref, b_ref, c_ref, d_ref, after_ref, o_ref):
        for i, ref in enumerate((a_ref, b_ref, c_ref, d_ref)):
            o_ref[i * RANK : (i + 1) * RANK, :] = ref[...]

    return pl.pallas_call(
        body,
        in_specs=[SCALARS] + [WHOLE] * 4 + [HBM],
        out_specs=WHOLE,
        out_shape=jax.ShapeDtypeStruct((4 * RANK, ROWS_OWN // 2), F32),
        cost_estimate=SMALL,
        compiler_params=params(),
        name="stack_early",
    )(place, *parts, after)


def assemble_left(place, own, oth):
    def body(place_ref, own_ref, oth_ref, o_ref, sum_ref):
        core, half = place_ref[2], ROWS_OWN // 2
        for y in range(4):
            rows = slice(y * RANK, (y + 1) * RANK)
            sum_ref[:, cut(2 * y + core, half)] = own_ref[rows, :]
            sum_ref[:, cut(2 * y + 1 - core, half)] = oth_ref[rows, :]
        for y in range(4):
            for x in range(4):
                i = 4 * y + x
                o_ref[:, i * PIECE : (i + 1) * PIECE] = sum_ref[:, cut(4 * y + (place_ref[1] ^ x), PIECE)]

    shape = jax.ShapeDtypeStruct((RANK, ROWS), F32)
    return call(body, "assemble_left", shape, place, own, oth, scratch=[pltpu.VMEM((RANK, ROWS), F32)], cost=SMALL)


def thirds(x):
    high = x.astype(BF)
    rest = x - high.astype(F32)
    mid = rest.astype(BF)
    low = (rest - mid.astype(F32)).astype(BF)
    return jnp.concatenate([high, mid, low], axis=0)


def dot(a, b, dims, precision=None):
    return lax.dot_general(a, b, ((dims[0], dims[1]), ((), ())), precision=precision, preferred_element_type=F32)


def thirds(x):
    high = x.astype(BF)
    rest = x - high.astype(F32)
    mid = rest.astype(BF)
    low = (rest - mid.astype(F32)).astype(BF)
    return jnp.concatenate([high, mid, low], axis=0)


def add_thirds(x):
    return x[:RANK] + (x[RANK : 2 * RANK] + x[2 * RANK :])


def reorder(rows, place_ref):
    blocks = [rows[:, i * PIECE : (i + 1) * PIECE] for i in range(16)]
    swapped = jnp.concatenate([blocks[(i % 4) * 4 + i // 4] for i in range(16)], axis=1)
    return jnp.where(place_ref[2] == 0, rows, swapped)


def store_halves(place_ref, left, own_ref, oth_ref):
    left = reorder(left, place_ref)
    low, high = left[:, :MID], left[:, MID:]
    first = place_ref[2] == 0
    own_ref[...] = jnp.where(first, low, high)
    oth_ref[...] = jnp.where(first, high, low)


def load_halves(place_ref, own_ref, oth_ref):
    first = place_ref[2] == 0
    own, oth = own_ref[...], oth_ref[...]
    return jnp.concatenate([jnp.where(first, own, oth), jnp.where(first, oth, own)], axis=1)


def times_m(rows, m_refs):
    parts = [dot(rows[:, i * ROWS_OWN : (i + 1) * ROWS_OWN], ref[...], ((1,), (0,))) for i, ref in enumerate(m_refs)]
    return (parts[0] + parts[1]) + (parts[2] + parts[3])


def times_m_t(rows, m_refs):
    return jnp.concatenate([dot(rows, ref[...], ((1,), (1,))) for ref in m_refs], axis=1)


def inverse_factor(gram):
    row = lax.broadcasted_iota(jnp.int32, (RANK, 128), 0)
    lane = lax.broadcasted_iota(jnp.int32, (RANK, 128), 1)
    wide = jnp.concatenate([gram, jnp.zeros((RANK, 128 - RANK), F32)], axis=1)
    trace = jnp.sum(jnp.where(row == lane, wide, 0.0), keepdims=True)
    shift = 1e-06 * (trace / RANK)
    work = wide + jnp.where(row == lane, shift, 0.0) + jnp.where(row + RANK == lane, 1.0, 0.0)
    for start in range(0, RANK, PANEL):
        cols = [jnp.broadcast_to(work[:, start + j : start + j + 1], (RANK, 128)) for j in range(PANEL)]
        for j in range(PANEL):
            k = start + j
            factor = jnp.where(row > k, cols[j] * (1.0 / cols[j][k : k + 1, :]), 0.0)
            work = work - factor * work[k : k + 1, :]
            for i in range(j + 1, PANEL):
                cols[i] = cols[i] - factor * cols[i][k : k + 1, :]
    pivot = jnp.sum(jnp.where(row == lane, work, 0.0), axis=1, keepdims=True)
    return work[:, RANK : 2 * RANK] * lax.rsqrt(pivot)


HALVES = [jax.ShapeDtypeStruct((RANK, MID), F32)] * 2


def from_left(place_ref, left, m_refs, own_ref, oth_ref):
    right = add_thirds(times_m(thirds(reorder(left, place_ref)), m_refs))
    store_halves(place_ref, add_thirds(times_m_t(thirds(right), m_refs)), own_ref, oth_ref)


def second_left(place, left, m):
    def body(place_ref, left_ref, m0, m1, m2, m3, own_ref, oth_ref):
        from_left(place_ref, left_ref[...], (m0, m1, m2, m3), own_ref, oth_ref)

    return call(body, "second_left", HALVES, place, left, *m)


def next_left(place, own, oth, inverse, m):
    def body(place_ref, own_in, oth_in, inv_ref, m0, m1, m2, m3, left_ref, own_ref, oth_ref):
        left = load_halves(place_ref, own_in, oth_in)
        left = dot(inv_ref[...], left, ((1,), (0,)), HIGHEST) * (1.0 / N_DP)
        left_ref[...] = left
        from_left(place_ref, left, (m0, m1, m2, m3), own_ref, oth_ref)

    shapes = [jax.ShapeDtypeStruct((RANK, ROWS), F32)] + HALVES
    return call(body, "next_left", shapes, place, own, oth, inverse, *m)


def inverse_of(place, left):
    def body(place_ref, left_ref, o_ref):
        left = left_ref[...]
        o_ref[...] = inverse_factor(dot(left, left, ((1,), (1,)), HIGHEST))

    return call(body, "inverse_of", jax.ShapeDtypeStruct((RANK, RANK), F32), place, left, cost=SMALL)


def last_right(place, own, oth, inverse, m):
    def body(place_ref, own_in, oth_in, inv_ref, m0, m1, m2, m3, right_ref, left_ref, out_ref):
        left = load_halves(place_ref, own_in, oth_in)
        left = dot(inv_ref[...], left, ((1,), (0,)), HIGHEST) * (1.0 / N_DP)
        raw = add_thirds(times_m(thirds(reorder(left, place_ref)), (m0, m1, m2, m3)))
        inverse = inverse_factor(dot(left, left, ((1,), (1,)), HIGHEST))
        right_ref[...] = dot(inverse, raw, ((1,), (0,)), HIGHEST) * (1.0 / N_DP)
        for k in range(4):
            left_ref[:, cut(place_ref[1] ^ k, PIECE)] = left[:, k * PIECE : (k + 1) * PIECE]
        out_ref[...] = inverse

    shapes = [(RANK, COLS), (RANK, ROWS_OWN), (RANK, RANK)]
    return call(body, "last_right", [jax.ShapeDtypeStruct(s, F32) for s in shapes], place, own, oth, inverse, *m)


def sum_over_group(own, oth, beside=None):
    own = own + lax.ppermute(oth, "dp", CORE)
    parts = spread(own, "z", "z")
    if beside is not None:
        parts, beside = lax.optimization_barrier((parts, beside))
    a, b, c, d = parts
    own = (a + b) + (c + d)
    return own, lax.ppermute(own, "dp", CORE), beside


def columns_of(place, left, inverse):
    def body(place_ref, left_ref, inv_ref, out_ref):
        ortho = dot(inv_ref[...], left_ref[...], ((1,), (0,)), HIGHEST)
        wide = jnp.concatenate([ortho] * 3 + [jnp.zeros((RANK, ROWS_OWN), F32)], axis=0)
        out_ref[...] = wide.T.astype(BF)

    return call(body, "columns_of", jax.ShapeDtypeStruct((ROWS_OWN, 4 * RANK), BF), place, left, inverse)


def finish(place, ortho, rights, mine, other, outs, name):
    keys = list(rights)
    count, kept = len(keys), len(outs)

    def body(place_ref, o_ref, *refs):
        rights, memory, refs = refs[:count], refs[count : count + 2], refs[count + 2 + kept :]
        up_hbm, err_hbm, right_hbm, up_ref, err_ref, sems = refs
        copies = []

        def send(i, n, source, target):
            copies.append(pltpu.make_async_copy(source, target, sems.at[i, n]))
            copies[-1].start()

        for n, ((k, j), ref) in enumerate(zip(keys, rights)):
            z = place_ref[0] ^ k
            cols = cut((place_ref[2] ^ j) * 4 + z, COLS)
            wide = jnp.concatenate([thirds(ref[...]), jnp.zeros((RANK, COLS), BF)], axis=0)
            update = dot(o_ref[...], wide, ((1,), (0,)))
            up_ref[n] = update
            send(0, n, up_ref.at[n], up_hbm.at[:, cols])
            err_ref[n] = memory[j][:, cut(z, COLS)].astype(F32) - update
            send(1, n, err_ref.at[n], err_hbm.at[:, cols])
            send(2, n, ref, right_hbm.at[:, cols])
        for copy in copies:
            copy.wait()

    blocks = pltpu.VMEM((count, ROWS_OWN, COLS), F32)
    return pl.pallas_call(
        body,
        in_specs=[SCALARS] + [WHOLE] * (count + 3) + [HBM] * kept,
        out_specs=[HBM] * 3,
        scratch_shapes=[blocks, blocks, pltpu.SemaphoreType.DMA((3, count))],
        out_shape=(
            jax.ShapeDtypeStruct((ROWS_OWN, W), F32),
            jax.ShapeDtypeStruct((ROWS_OWN, W), F32),
            jax.ShapeDtypeStruct((RANK, W), F32),
        ),
        input_output_aliases={count + 4 + i: i for i in range(kept)},
        compiler_params=params(),
        name=name,
    )(place, ortho, *rights.values(), mine, other, *outs)


def per_device(grad, error, warm_right):
    dp = lax.axis_index("dp")
    core = dp & 1
    place = jnp.stack([dp >> 3, (dp >> 1) & 3, core]).astype(jnp.int32)

    other = half_of_memory(grad[0], error[0], (1 - core)[None])
    received = lax.ppermute(other, "dp", CORE)
    mine = half_of_memory(grad[0], error[0], core[None])
    pairs = pair_sum(place, mine, received)
    early, passed = early_left(place, warm_right.T, pairs)
    early = early + lax.ppermute(passed, "dp", CORE)
    parts, early = lax.optimization_barrier((exchange(pairs, "z", "x"), spread(early, "y", "y")))
    rows = first_sum(place, parts)
    early = spread(stack_early(place, early, rows[0]), "z", "x")
    parts, early = lax.optimization_barrier((exchange(rows, "x", "z"), early))
    piece = second_sum(place, parts)
    early = spread((early[0] + early[1]) + (early[2] + early[3]), "x", "z")
    m = jnp.concatenate(spread(piece, "x", "y"), axis=0)
    early = (early[0] + early[1]) + (early[2] + early[3])
    left = assemble_left(place, early, lax.ppermute(early, "dp", CORE))
    m = spread(m, "y", "x")
    m, left = lax.optimization_barrier((m, left))

    own, oth, inverse = sum_over_group(*second_left(place, left, m), inverse_of(place, left))
    for step in range(ITERS - 2):
        left, own, oth = next_left(place, own, oth, inverse, m)
        own, oth, inverse = sum_over_group(own, oth, inverse_of(place, left))
    right, left, inverse = last_right(place, own, oth, inverse, m)

    ortho = columns_of(place, left, inverse)
    near = {(0, 0): right, (0, 1): lax.ppermute(right, "dp", CORE)}
    outs = finish(place, ortho, near, mine, other, [], "finish_near")
    rights, outs = lax.optimization_barrier((spread(right, "z", "z"), outs))
    far = {(k, 0): rights[k] for k in (1, 2, 3)}
    far.update({(k, 1): lax.ppermute(rights[k], "dp", CORE) for k in (1, 2, 3)})
    update, new_error, right_t = finish(place, ortho, far, mine, other, outs, "finish_far")
    return update, new_error[None], right_t.T


def solution(mesh):
    placed = (P("dp", "owner", None), P("dp", "owner", None), P())
    return jax.shard_map(
        per_device,
        mesh=mesh,
        in_specs=placed,
        out_specs=(P("owner", None), P("dp", "owner", None), P()),
        check_vma=False,
    )
```

```python
import jax
import jax.numpy as jnp
from jax import lax
from jax.experimental import pallas as pl
from jax.experimental.pallas import tpu as pltpu
from jax.sharding import PartitionSpec as P

W = 4096
RANK = 32
ITERS = 4
ROWS = 2048
N_DP = 32
N_OWNER = 4
HALF = W // 2
COLS = HALF // 4
ROWS_OWN = ROWS // N_OWNER
PIECE = ROWS_OWN // 4
MID = ROWS // 2
PANEL = 8
BF = jnp.bfloat16
F32 = jnp.float32
HIGHEST = lax.Precision.HIGHEST

CORE = [(i, i ^ 1) for i in range(N_DP)]
STEP = {"z": 32, "x": 8, "y": 1}


def along(array, first, second, k):
    step = (STEP[first], STEP[second])
    pairs = [(i, i ^ (k * step[(i >> 2) & 1])) for i in range(N_DP * N_OWNER)]
    return lax.ppermute(array, ("dp", "owner"), pairs)


def exchange(arrays, first, second):
    return [arrays[0]] + [along(arrays[k], first, second, k) for k in (1, 2, 3)]


def spread(array, first, second):
    return exchange([array] * 4, first, second)


def params(**kw):
    return pltpu.CompilerParams(vmem_limit_bytes=48 * 1024 * 1024, **kw)


SCALARS = pl.BlockSpec(memory_space=pltpu.SMEM)
WHOLE = pl.BlockSpec(memory_space=pltpu.VMEM)
HBM = pl.BlockSpec(memory_space=pl.ANY)
SMALL = pl.CostEstimate(flops=1000, bytes_accessed=1000, transcendentals=0)


def half_of_memory(grad, error, which):
    chunks = 8
    rows = ROWS_OWN // chunks

    def body(which_ref, g_hbm, e_hbm, o_ref, g_ref, e_ref, sems):
        cols = cut(which_ref[0], HALF)
        copies = []
        for i in range(chunks):
            part = pl.ds(i * rows, rows)
            pair = [
                pltpu.make_async_copy(src.at[part, cols], dst.at[part, :], sems.at[n, i])
                for n, (src, dst) in enumerate(((g_hbm, g_ref), (e_hbm, e_ref)))
            ]
            for copy in pair:
                copy.start()
            copies.append(pair)
        for i, pair in enumerate(copies):
            for copy in pair:
                copy.wait()
            part = pl.ds(i * rows, rows)
            o_ref[part, :] = (g_ref[part, :].astype(F32) + e_ref[part, :].astype(F32)).astype(BF)

    return pl.pallas_call(
        body,
        in_specs=[SCALARS, HBM, HBM],
        out_specs=WHOLE,
        scratch_shapes=[pltpu.VMEM((ROWS_OWN, HALF), BF)] * 2 + [pltpu.SemaphoreType.DMA((2, chunks))],
        out_shape=jax.ShapeDtypeStruct((ROWS_OWN, HALF), BF),
        compiler_params=params(),
        name="half_of_memory",
    )(which, grad, error)


def call(body, name, out_shape, place, *arrays, scratch=(), cost=None):
    return pl.pallas_call(
        body,
        in_specs=[SCALARS] + [WHOLE] * len(arrays),
        out_specs=jax.tree.map(lambda s: WHOLE, out_shape),
        out_shape=out_shape,
        scratch_shapes=scratch,
        cost_estimate=cost,
        compiler_params=params(),
        name=name,
    )(place, *arrays)


def cut(index, size):
    return pl.ds(pl.multiple_of(index * size, size), size)


def pair_sum(place, mine, received):
    def body(place_ref, a_ref, b_ref, *out):
        first = place_ref[2] == 0
        for k in range(4):
            for j in range(4):
                rows = cut(jnp.where(first, j, place_ref[1] ^ k), PIECE)
                cols = cut(jnp.where(first, place_ref[0] ^ k, j), COLS)
                out[k][j] = a_ref[rows, cols] + b_ref[rows, cols]

    return call(body, "pair_sum", [jax.ShapeDtypeStruct((4, PIECE, COLS), BF)] * 4, place, mine, received)


def first_sum(place, parts):
    def body(place_ref, *refs):
        own = jnp.where(place_ref[2] == 0, place_ref[1], place_ref[0])
        for k in range(4):
            total = refs[0][own ^ k].astype(F32)
            for ref in refs[1:4]:
                total = total + ref[own ^ k].astype(F32)
            refs[4 + k][...] = total.astype(BF)

    return call(body, "first_sum", [jax.ShapeDtypeStruct((PIECE, COLS), BF)] * 4, place, *parts)


def second_sum(place, parts):
    def body(place_ref, a_ref, b_ref, c_ref, d_ref, o_ref):
        total = a_ref[...].astype(F32) + b_ref[...].astype(F32)
        o_ref[...] = (total + (c_ref[...].astype(F32) + d_ref[...].astype(F32))).astype(BF)

    return call(body, "second_sum", jax.ShapeDtypeStruct((PIECE, COLS), BF), place, *parts)


def early_left(place, warm_t, pairs):
    def body(place_ref, warm_ref, *refs):
        pairs, (own_ref, oth_ref, sum_ref) = refs[:4], refs[4:]
        core = place_ref[2]
        sum_ref[...] = jnp.zeros((RANK, ROWS_OWN), F32)
        for k in range(4):
            for j in range(4):
                rows = cut(jnp.where(core == 0, j, place_ref[1] ^ k), PIECE)
                group = jnp.where(core == 0, place_ref[0] ^ k, j)
                right = warm_ref[:, cut(core * 4 + group, COLS)].astype(BF)
                sum_ref[:, rows] += dot(right, pairs[k][j], ((1,), (1,)))
        own_ref[...] = sum_ref[:, cut(core, ROWS_OWN // 2)]
        oth_ref[...] = sum_ref[:, cut(1 - core, ROWS_OWN // 2)]

    shapes = [jax.ShapeDtypeStruct((RANK, ROWS_OWN // 2), F32)] * 2
    scratch = [pltpu.VMEM((RANK, ROWS_OWN), F32)]
    return call(body, "early_left", shapes, place, warm_t, *pairs, scratch=scratch)


def stack_early(place, parts):
    def body(place_ref, a_ref, b_ref, c_ref, d_ref, o_ref):
        for i, ref in enumerate((a_ref, b_ref, c_ref, d_ref)):
            o_ref[i * RANK : (i + 1) * RANK, :] = ref[...]

    return call(body, "stack_early", jax.ShapeDtypeStruct((4 * RANK, ROWS_OWN // 2), F32), place, *parts)


def assemble_left(place, own, oth):
    def body(place_ref, own_ref, oth_ref, o_ref, sum_ref):
        core, half = place_ref[2], ROWS_OWN // 2
        for y in range(4):
            rows = slice(y * RANK, (y + 1) * RANK)
            sum_ref[:, cut(2 * y + core, half)] = own_ref[rows, :]
            sum_ref[:, cut(2 * y + 1 - core, half)] = oth_ref[rows, :]
        for y in range(4):
            for x in range(4):
                i = 4 * y + x
                o_ref[:, i * PIECE : (i + 1) * PIECE] = sum_ref[:, cut(4 * y + (place_ref[1] ^ x), PIECE)]

    shape = jax.ShapeDtypeStruct((RANK, ROWS), F32)
    return call(body, "assemble_left", shape, place, own, oth, scratch=[pltpu.VMEM((RANK, ROWS), F32)], cost=SMALL)


def thirds(x):
    high = x.astype(BF)
    rest = x - high.astype(F32)
    mid = rest.astype(BF)
    low = (rest - mid.astype(F32)).astype(BF)
    return jnp.concatenate([high, mid, low], axis=0)


def dot(a, b, dims, precision=None):
    return lax.dot_general(a, b, ((dims[0], dims[1]), ((), ())), precision=precision, preferred_element_type=F32)


def thirds(x):
    high = x.astype(BF)
    rest = x - high.astype(F32)
    mid = rest.astype(BF)
    low = (rest - mid.astype(F32)).astype(BF)
    return jnp.concatenate([high, mid, low], axis=0)


def add_thirds(x):
    return x[:RANK] + (x[RANK : 2 * RANK] + x[2 * RANK :])


def reorder(rows, place_ref):
    blocks = [rows[:, i * PIECE : (i + 1) * PIECE] for i in range(16)]
    swapped = jnp.concatenate([blocks[(i % 4) * 4 + i // 4] for i in range(16)], axis=1)
    return jnp.where(place_ref[2] == 0, rows, swapped)


def store_halves(place_ref, left, own_ref, oth_ref):
    left = reorder(left, place_ref)
    low, high = left[:, :MID], left[:, MID:]
    first = place_ref[2] == 0
    own_ref[...] = jnp.where(first, low, high)
    oth_ref[...] = jnp.where(first, high, low)


def load_halves(place_ref, own_ref, oth_ref):
    first = place_ref[2] == 0
    own, oth = own_ref[...], oth_ref[...]
    return jnp.concatenate([jnp.where(first, own, oth), jnp.where(first, oth, own)], axis=1)


def times_m(rows, m_refs):
    parts = [dot(rows[:, i * ROWS_OWN : (i + 1) * ROWS_OWN], ref[...], ((1,), (0,))) for i, ref in enumerate(m_refs)]
    return (parts[0] + parts[1]) + (parts[2] + parts[3])


def times_m_t(rows, m_refs):
    return jnp.concatenate([dot(rows, ref[...], ((1,), (1,))) for ref in m_refs], axis=1)


def inverse_factor(gram):
    row = lax.broadcasted_iota(jnp.int32, (RANK, 128), 0)
    lane = lax.broadcasted_iota(jnp.int32, (RANK, 128), 1)
    wide = jnp.concatenate([gram, jnp.zeros((RANK, 128 - RANK), F32)], axis=1)
    trace = jnp.sum(jnp.where(row == lane, wide, 0.0), keepdims=True)
    shift = 1e-06 * (trace / RANK)
    work = wide + jnp.where(row == lane, shift, 0.0) + jnp.where(row + RANK == lane, 1.0, 0.0)
    for start in range(0, RANK, PANEL):
        cols = [jnp.broadcast_to(work[:, start + j : start + j + 1], (RANK, 128)) for j in range(PANEL)]
        for j in range(PANEL):
            k = start + j
            factor = jnp.where(row > k, cols[j] * (1.0 / cols[j][k : k + 1, :]), 0.0)
            work = work - factor * work[k : k + 1, :]
            for i in range(j + 1, PANEL):
                cols[i] = cols[i] - factor * cols[i][k : k + 1, :]
    pivot = jnp.sum(jnp.where(row == lane, work, 0.0), axis=1, keepdims=True)
    return work[:, RANK : 2 * RANK] * lax.rsqrt(pivot)


HALVES = [jax.ShapeDtypeStruct((RANK, MID), F32)] * 2


def from_left(place_ref, left, m_refs, own_ref, oth_ref):
    right = add_thirds(times_m(thirds(reorder(left, place_ref)), m_refs))
    store_halves(place_ref, add_thirds(times_m_t(thirds(right), m_refs)), own_ref, oth_ref)


def second_left(place, left, m):
    def body(place_ref, left_ref, m0, m1, m2, m3, own_ref, oth_ref):
        from_left(place_ref, left_ref[...], (m0, m1, m2, m3), own_ref, oth_ref)

    return call(body, "second_left", HALVES, place, left, *m)


def next_left(place, own, oth, inverse, m):
    def body(place_ref, own_in, oth_in, inv_ref, m0, m1, m2, m3, left_ref, own_ref, oth_ref):
        left = load_halves(place_ref, own_in, oth_in)
        left = dot(inv_ref[...], left, ((1,), (0,)), HIGHEST) * (1.0 / N_DP)
        left_ref[...] = left
        from_left(place_ref, left, (m0, m1, m2, m3), own_ref, oth_ref)

    shapes = [jax.ShapeDtypeStruct((RANK, ROWS), F32)] + HALVES
    return call(body, "next_left", shapes, place, own, oth, inverse, *m)


def inverse_of(place, left):
    def body(place_ref, left_ref, o_ref):
        left = left_ref[...]
        o_ref[...] = inverse_factor(dot(left, left, ((1,), (1,)), HIGHEST))

    return call(body, "inverse_of", jax.ShapeDtypeStruct((RANK, RANK), F32), place, left, cost=SMALL)


def last_right(place, own, oth, inverse, m):
    def body(place_ref, own_in, oth_in, inv_ref, m0, m1, m2, m3, right_ref, left_ref, out_ref):
        left = load_halves(place_ref, own_in, oth_in)
        left = dot(inv_ref[...], left, ((1,), (0,)), HIGHEST) * (1.0 / N_DP)
        raw = add_thirds(times_m(thirds(reorder(left, place_ref)), (m0, m1, m2, m3)))
        inverse = inverse_factor(dot(left, left, ((1,), (1,)), HIGHEST))
        right_ref[...] = (dot(inverse, raw, ((1,), (0,)), HIGHEST) * (1.0 / N_DP)).astype(BF)
        for k in range(4):
            left_ref[:, cut(place_ref[1] ^ k, PIECE)] = left[:, k * PIECE : (k + 1) * PIECE]
        out_ref[...] = inverse

    shapes = [((RANK, COLS), BF), ((RANK, ROWS_OWN), F32), ((RANK, RANK), F32)]
    return call(body, "last_right", [jax.ShapeDtypeStruct(*s) for s in shapes], place, own, oth, inverse, *m)


def sum_over_group(own, oth, beside=None):
    own = own + lax.ppermute(oth, "dp", CORE)
    parts = spread(own, "z", "z")
    if beside is not None:
        parts, beside = lax.optimization_barrier((parts, beside))
    a, b, c, d = parts
    own = (a + b) + (c + d)
    return own, lax.ppermute(own, "dp", CORE), beside


def columns_of(place, left, inverse):
    def body(place_ref, left_ref, inv_ref, out_ref):
        out_ref[...] = dot(inv_ref[...], left_ref[...], ((1,), (0,)), HIGHEST).T.astype(BF)

    return call(body, "columns_of", jax.ShapeDtypeStruct((ROWS_OWN, RANK), BF), place, left, inverse)


def finish(place, ortho, rights, mine, other, outs, name):
    keys = list(rights)
    count, kept = len(keys), len(outs)

    def body(place_ref, o_ref, *refs):
        rights, memory, refs = refs[:count], refs[count : count + 2], refs[count + 2 + kept :]
        up_hbm, err_hbm, right_hbm, up_ref, err_ref, right_ref, sems = refs
        copies = []

        def send(i, n, source, target):
            copies.append(pltpu.make_async_copy(source, target, sems.at[i, n]))
            copies[-1].start()

        for n, ((k, j), ref) in enumerate(zip(keys, rights)):
            z = place_ref[0] ^ k
            cols = cut((place_ref[2] ^ j) * 4 + z, COLS)
            update = dot(o_ref[...], ref[...], ((1,), (0,)))
            up_ref[n] = update
            send(0, n, up_ref.at[n], up_hbm.at[:, cols])
            err_ref[n] = memory[j][:, cut(z, COLS)].astype(F32) - update
            send(1, n, err_ref.at[n], err_hbm.at[:, cols])
            right_ref[n] = ref[...].astype(F32)
            send(2, n, right_ref.at[n], right_hbm.at[:, cols])
        for copy in copies:
            copy.wait()

    blocks = pltpu.VMEM((count, ROWS_OWN, COLS), F32)
    return pl.pallas_call(
        body,
        in_specs=[SCALARS] + [WHOLE] * (count + 3) + [HBM] * kept,
        out_specs=[HBM] * 3,
        scratch_shapes=[blocks, blocks, pltpu.VMEM((count, RANK, COLS), F32), pltpu.SemaphoreType.DMA((3, count))],
        out_shape=(
            jax.ShapeDtypeStruct((ROWS_OWN, W), F32),
            jax.ShapeDtypeStruct((ROWS_OWN, W), F32),
            jax.ShapeDtypeStruct((RANK, W), F32),
        ),
        input_output_aliases={count + 4 + i: i for i in range(kept)},
        compiler_params=params(),
        name=name,
    )(place, ortho, *rights.values(), mine, other, *outs)


def per_device(grad, error, warm_right):
    dp = lax.axis_index("dp")
    core = dp & 1
    place = jnp.stack([dp >> 3, (dp >> 1) & 3, core]).astype(jnp.int32)

    other = half_of_memory(grad[0], error[0], (1 - core)[None])
    received = lax.ppermute(other, "dp", CORE)
    mine = half_of_memory(grad[0], error[0], core[None])
    pairs = pair_sum(place, mine, received)
    early, passed = early_left(place, warm_right.T, pairs)
    early = early + lax.ppermute(passed, "dp", CORE)
    early = stack_early(place, spread(early, "y", "y"))
    parts, early = lax.optimization_barrier((exchange(pairs, "z", "x"), early))
    rows = first_sum(place, parts)
    early = spread(early, "z", "x")
    parts, early = lax.optimization_barrier((exchange(rows, "x", "z"), early))
    piece = second_sum(place, parts)
    early = spread((early[0] + early[1]) + (early[2] + early[3]), "x", "z")
    m = jnp.concatenate(spread(piece, "x", "y"), axis=0)
    early = (early[0] + early[1]) + (early[2] + early[3])
    left = assemble_left(place, early, lax.ppermute(early, "dp", CORE))
    m = spread(m, "y", "x")
    m, left = lax.optimization_barrier((m, left))

    own, oth, inverse = sum_over_group(*second_left(place, left, m), inverse_of(place, left))
    for step in range(ITERS - 2):
        left, own, oth = next_left(place, own, oth, inverse, m)
        own, oth, inverse = sum_over_group(own, oth, inverse_of(place, left))
    right, left, inverse = last_right(place, own, oth, inverse, m)

    ortho = columns_of(place, left, inverse)
    near = {(0, 0): right, (0, 1): lax.ppermute(right, "dp", CORE)}
    outs = finish(place, ortho, near, mine, other, [], "finish_near")
    rights, outs = lax.optimization_barrier((spread(right, "z", "z"), outs))
    far = {(k, 0): rights[k] for k in (1, 2, 3)}
    far.update({(k, 1): lax.ppermute(rights[k], "dp", CORE) for k in (1, 2, 3)})
    update, new_error, right_t = finish(place, ortho, far, mine, other, outs, "finish_far")
    return update, new_error[None], right_t.T


def solution(mesh):
    placed = (P("dp", "owner", None), P("dp", "owner", None), P())
    return jax.shard_map(
        per_device,
        mesh=mesh,
        in_specs=placed,
        out_specs=(P("owner", None), P("dp", "owner", None), P()),
        check_vma=False,
    )
```

```python
import jax
import jax.numpy as jnp
from jax import lax
from jax.experimental import pallas as pl
from jax.experimental.pallas import tpu as pltpu
from jax.sharding import PartitionSpec as P

W = 4096
RANK = 32
ITERS = 4
ROWS = 2048
N_DP = 32
N_OWNER = 4
HALF = W // 2
COLS = HALF // 4
ROWS_OWN = ROWS // N_OWNER
PIECE = ROWS_OWN // 4
MID = ROWS // 2
PANEL = 16
BF = jnp.bfloat16
F32 = jnp.float32
HIGHEST = lax.Precision.HIGHEST

CORE = [(i, i ^ 1) for i in range(N_DP)]
STEP = {"z": 32, "x": 8, "y": 1}


def along(array, first, second, k):
    step = (STEP[first], STEP[second])
    pairs = [(i, i ^ (k * step[(i >> 2) & 1])) for i in range(N_DP * N_OWNER)]
    return lax.ppermute(array, ("dp", "owner"), pairs)


def exchange(arrays, first, second):
    return [arrays[0]] + [along(arrays[k], first, second, k) for k in (1, 2, 3)]


def spread(array, first, second):
    return exchange([array] * 4, first, second)


def params(**kw):
    return pltpu.CompilerParams(vmem_limit_bytes=48 * 1024 * 1024, **kw)


SCALARS = pl.BlockSpec(memory_space=pltpu.SMEM)
WHOLE = pl.BlockSpec(memory_space=pltpu.VMEM)
HBM = pl.BlockSpec(memory_space=pl.ANY)
SMALL = pl.CostEstimate(flops=1000, bytes_accessed=1000, transcendentals=0)


def half_of_memory(grad, error, which):
    chunks = 8
    rows = ROWS_OWN // chunks

    def body(which_ref, g_hbm, e_hbm, o_ref, g_ref, e_ref, sems):
        cols = cut(which_ref[0], HALF)
        copies = []
        for i in range(chunks):
            part = pl.ds(i * rows, rows)
            pair = [
                pltpu.make_async_copy(src.at[part, cols], dst.at[part, :], sems.at[n, i])
                for n, (src, dst) in enumerate(((g_hbm, g_ref), (e_hbm, e_ref)))
            ]
            for copy in pair:
                copy.start()
            copies.append(pair)
        for i, pair in enumerate(copies):
            for copy in pair:
                copy.wait()
            part = pl.ds(i * rows, rows)
            o_ref[part, :] = (g_ref[part, :].astype(F32) + e_ref[part, :].astype(F32)).astype(BF)

    return pl.pallas_call(
        body,
        in_specs=[SCALARS, HBM, HBM],
        out_specs=WHOLE,
        scratch_shapes=[pltpu.VMEM((ROWS_OWN, HALF), BF)] * 2 + [pltpu.SemaphoreType.DMA((2, chunks))],
        out_shape=jax.ShapeDtypeStruct((ROWS_OWN, HALF), BF),
        compiler_params=params(),
        name="half_of_memory",
    )(which, grad, error)


def call(body, name, out_shape, place, *arrays, scratch=(), cost=None):
    return pl.pallas_call(
        body,
        in_specs=[SCALARS] + [WHOLE] * len(arrays),
        out_specs=jax.tree.map(lambda s: WHOLE, out_shape),
        out_shape=out_shape,
        scratch_shapes=scratch,
        cost_estimate=cost,
        compiler_params=params(),
        name=name,
    )(place, *arrays)


def cut(index, size):
    return pl.ds(pl.multiple_of(index * size, size), size)


def pair_sum(place, mine, received):
    def body(place_ref, a_ref, b_ref, *out):
        first = place_ref[2] == 0
        for k in range(4):
            for j in range(4):
                rows = cut(jnp.where(first, j, place_ref[1] ^ k), PIECE)
                cols = cut(jnp.where(first, place_ref[0] ^ k, j), COLS)
                out[k][j] = a_ref[rows, cols] + b_ref[rows, cols]

    return call(body, "pair_sum", [jax.ShapeDtypeStruct((4, PIECE, COLS), BF)] * 4, place, mine, received)


def first_sum(place, parts):
    def body(place_ref, *refs):
        own = jnp.where(place_ref[2] == 0, place_ref[1], place_ref[0])
        for k in range(4):
            total = refs[0][own ^ k].astype(F32)
            for ref in refs[1:4]:
                total = total + ref[own ^ k].astype(F32)
            refs[4 + k][...] = total.astype(BF)

    return call(body, "first_sum", [jax.ShapeDtypeStruct((PIECE, COLS), BF)] * 4, place, *parts)


def second_sum(place, parts):
    def body(place_ref, a_ref, b_ref, c_ref, d_ref, o_ref):
        total = a_ref[...].astype(F32) + b_ref[...].astype(F32)
        o_ref[...] = (total + (c_ref[...].astype(F32) + d_ref[...].astype(F32))).astype(BF)

    return call(body, "second_sum", jax.ShapeDtypeStruct((PIECE, COLS), BF), place, *parts)


def early_left(place, warm_t, pairs):
    def body(place_ref, warm_ref, *refs):
        pairs, (own_ref, oth_ref, sum_ref) = refs[:4], refs[4:]
        core = place_ref[2]
        sum_ref[...] = jnp.zeros((RANK, ROWS_OWN), F32)
        for k in range(4):
            for j in range(4):
                rows = cut(jnp.where(core == 0, j, place_ref[1] ^ k), PIECE)
                group = jnp.where(core == 0, place_ref[0] ^ k, j)
                right = warm_ref[:, cut(core * 4 + group, COLS)].astype(BF)
                sum_ref[:, rows] += dot(right, pairs[k][j], ((1,), (1,)))
        own_ref[...] = sum_ref[:, cut(core, ROWS_OWN // 2)]
        oth_ref[...] = sum_ref[:, cut(1 - core, ROWS_OWN // 2)]

    shapes = [jax.ShapeDtypeStruct((RANK, ROWS_OWN // 2), F32)] * 2
    scratch = [pltpu.VMEM((RANK, ROWS_OWN), F32)]
    return call(body, "early_left", shapes, place, warm_t, *pairs, scratch=scratch)


def stack_early(place, parts):
    def body(place_ref, a_ref, b_ref, c_ref, d_ref, o_ref):
        for i, ref in enumerate((a_ref, b_ref, c_ref, d_ref)):
            o_ref[i * RANK : (i + 1) * RANK, :] = ref[...]

    return call(body, "stack_early", jax.ShapeDtypeStruct((4 * RANK, ROWS_OWN // 2), F32), place, *parts)


def thirds(x):
    high = x.astype(BF)
    rest = x - high.astype(F32)
    mid = rest.astype(BF)
    low = (rest - mid.astype(F32)).astype(BF)
    return jnp.concatenate([high, mid, low], axis=0)


def dot(a, b, dims, precision=None):
    return lax.dot_general(a, b, ((dims[0], dims[1]), ((), ())), precision=precision, preferred_element_type=F32)


def thirds(x):
    high = x.astype(BF)
    rest = x - high.astype(F32)
    mid = rest.astype(BF)
    low = (rest - mid.astype(F32)).astype(BF)
    return jnp.concatenate([high, mid, low], axis=0)


def add_thirds(x):
    return x[:RANK] + (x[RANK : 2 * RANK] + x[2 * RANK :])


def reorder(rows, place_ref):
    blocks = [rows[:, i * PIECE : (i + 1) * PIECE] for i in range(16)]
    swapped = jnp.concatenate([blocks[(i % 4) * 4 + i // 4] for i in range(16)], axis=1)
    return jnp.where(place_ref[2] == 0, rows, swapped)


def store_halves(place_ref, left, own_ref, oth_ref):
    left = reorder(left, place_ref)
    low, high = left[:, :MID], left[:, MID:]
    first = place_ref[2] == 0
    own_ref[...] = jnp.where(first, low, high)
    oth_ref[...] = jnp.where(first, high, low)


def load_halves(place_ref, own_ref, oth_ref):
    first = place_ref[2] == 0
    own, oth = own_ref[...], oth_ref[...]
    return jnp.concatenate([jnp.where(first, own, oth), jnp.where(first, oth, own)], axis=1)


def times_m(rows, m_refs):
    parts = [dot(rows[:, i * ROWS_OWN : (i + 1) * ROWS_OWN], ref[...], ((1,), (0,))) for i, ref in enumerate(m_refs)]
    return (parts[0] + parts[1]) + (parts[2] + parts[3])


def times_m_t(rows, m_refs):
    return jnp.concatenate([dot(rows, ref[...], ((1,), (1,))) for ref in m_refs], axis=1)


def inverse_factor(gram):
    row = lax.broadcasted_iota(jnp.int32, (RANK, 128), 0)
    lane = lax.broadcasted_iota(jnp.int32, (RANK, 128), 1)
    wide = jnp.concatenate([gram, jnp.zeros((RANK, 128 - RANK), F32)], axis=1)
    trace = jnp.sum(jnp.where(row == lane, wide, 0.0), keepdims=True)
    shift = 1e-06 * (trace / RANK)
    work = wide + jnp.where(row == lane, shift, 0.0) + jnp.where(row + RANK == lane, 1.0, 0.0)
    for start in range(0, RANK, PANEL):
        cols = [jnp.broadcast_to(work[:, start + j : start + j + 1], (RANK, 128)) for j in range(PANEL)]
        for j in range(PANEL):
            k = start + j
            factor = jnp.where(row > k, cols[j] * (1.0 / cols[j][k : k + 1, :]), 0.0)
            work = work - factor * work[k : k + 1, :]
            for i in range(j + 1, PANEL):
                cols[i] = cols[i] - factor * cols[i][k : k + 1, :]
    pivot = jnp.sum(jnp.where(row == lane, work, 0.0), axis=1, keepdims=True)
    return work[:, RANK : 2 * RANK] * lax.rsqrt(pivot)


HALVES = [jax.ShapeDtypeStruct((RANK, MID), F32)] * 2


def from_left(place_ref, left, m_refs, own_ref, oth_ref):
    right = add_thirds(times_m(thirds(reorder(left, place_ref)), m_refs))
    store_halves(place_ref, add_thirds(times_m_t(thirds(right), m_refs)), own_ref, oth_ref)


def second_left(place, own, oth, m):
    def body(place_ref, own_in, oth_in, m0, m1, m2, m3, left_ref, own_ref, oth_ref, sum_ref):
        core, half = place_ref[2], ROWS_OWN // 2
        for y in range(4):
            rows = slice(y * RANK, (y + 1) * RANK)
            sum_ref[:, cut(2 * y + core, half)] = own_in[rows, :]
            sum_ref[:, cut(2 * y + 1 - core, half)] = oth_in[rows, :]
        for i in range(16):
            source = cut(i // 4 * 4 + (place_ref[1] ^ (i % 4)), PIECE)
            left_ref[:, i * PIECE : (i + 1) * PIECE] = sum_ref[:, source]
        from_left(place_ref, left_ref[...], (m0, m1, m2, m3), own_ref, oth_ref)

    shapes = [jax.ShapeDtypeStruct((RANK, ROWS), F32)] + HALVES
    return call(body, "second_left", shapes, place, own, oth, *m, scratch=[pltpu.VMEM((RANK, ROWS), F32)])


def next_left(place, own, oth, inverse, m):
    def body(place_ref, own_in, oth_in, inv_ref, m0, m1, m2, m3, left_ref, own_ref, oth_ref):
        left = load_halves(place_ref, own_in, oth_in)
        left = dot(inv_ref[...], left, ((1,), (0,)), HIGHEST) * (1.0 / N_DP)
        left_ref[...] = left
        from_left(place_ref, left, (m0, m1, m2, m3), own_ref, oth_ref)

    shapes = [jax.ShapeDtypeStruct((RANK, ROWS), F32)] + HALVES
    return call(body, "next_left", shapes, place, own, oth, inverse, *m)


def inverse_of(place, left):
    def body(place_ref, left_ref, o_ref):
        left = left_ref[...]
        o_ref[...] = inverse_factor(dot(left, left, ((1,), (1,)), HIGHEST))

    return call(body, "inverse_of", jax.ShapeDtypeStruct((RANK, RANK), F32), place, left, cost=SMALL)


def last_right(place, own, oth, inverse, m):
    def body(place_ref, own_in, oth_in, inv_ref, m0, m1, m2, m3, right_ref, left_ref, out_ref):
        left = load_halves(place_ref, own_in, oth_in)
        left = dot(inv_ref[...], left, ((1,), (0,)), HIGHEST) * (1.0 / N_DP)
        raw = add_thirds(times_m(thirds(reorder(left, place_ref)), (m0, m1, m2, m3)))
        inverse = inverse_factor(dot(left, left, ((1,), (1,)), HIGHEST))
        right_ref[...] = (dot(inverse, raw, ((1,), (0,)), HIGHEST) * (1.0 / N_DP)).astype(BF)
        for k in range(4):
            left_ref[:, cut(place_ref[1] ^ k, PIECE)] = left[:, k * PIECE : (k + 1) * PIECE]
        out_ref[...] = inverse

    shapes = [((RANK, COLS), BF), ((RANK, ROWS_OWN), F32), ((RANK, RANK), F32)]
    return call(body, "last_right", [jax.ShapeDtypeStruct(*s) for s in shapes], place, own, oth, inverse, *m)


def sum_over_group(own, oth, beside=None):
    own = own + lax.ppermute(oth, "dp", CORE)
    parts = spread(own, "z", "z")
    if beside is not None:
        parts, beside = lax.optimization_barrier((parts, beside))
    a, b, c, d = parts
    own = (a + b) + (c + d)
    return own, lax.ppermute(own, "dp", CORE), beside


def finish(place, ortho, rights, mine, other, outs, name):
    keys = list(rights)
    count, kept, made = len(keys), len(outs), len(ortho) == 2

    def body(place_ref, *refs):
        ortho_refs, refs = refs[: len(ortho)], refs[len(ortho) :]
        rights, memory, refs = refs[:count], refs[count : count + 2], refs[count + 2 + kept :]
        up_hbm, err_hbm, right_hbm = refs[:3]
        up_ref, err_ref, right_ref, sems = refs[-4:]
        o_ref = ortho_refs[0]
        if made:
            o_ref = refs[3]
            o_ref[...] = dot(ortho_refs[1][...], ortho_refs[0][...], ((1,), (0,)), HIGHEST).T.astype(BF)
        copies = []

        def send(i, n, source, target):
            copies.append(pltpu.make_async_copy(source, target, sems.at[i, n]))
            copies[-1].start()

        for n, ((k, j), ref) in enumerate(zip(keys, rights)):
            z = place_ref[0] ^ k
            cols = cut((place_ref[2] ^ j) * 4 + z, COLS)
            update = dot(o_ref[...], ref[...], ((1,), (0,)))
            up_ref[n] = update
            send(0, n, up_ref.at[n], up_hbm.at[:, cols])
            err_ref[n] = memory[j][:, cut(z, COLS)].astype(F32) - update
            send(1, n, err_ref.at[n], err_hbm.at[:, cols])
            right_ref[n] = ref[...].astype(F32)
            send(2, n, right_ref.at[n], right_hbm.at[:, cols])
        for copy in copies:
            copy.wait()

    blocks = pltpu.VMEM((count, ROWS_OWN, COLS), F32)
    return pl.pallas_call(
        body,
        in_specs=[SCALARS] + [WHOLE] * (len(ortho) + count + 2) + [HBM] * kept,
        out_specs=[HBM] * 3 + [WHOLE] * made,
        scratch_shapes=[blocks, blocks, pltpu.VMEM((count, RANK, COLS), F32), pltpu.SemaphoreType.DMA((3, count))],
        out_shape=(
            jax.ShapeDtypeStruct((ROWS_OWN, W), F32),
            jax.ShapeDtypeStruct((ROWS_OWN, W), F32),
            jax.ShapeDtypeStruct((RANK, W), F32),
        )
        + (jax.ShapeDtypeStruct((ROWS_OWN, RANK), BF),) * made,
        input_output_aliases={count + 4 + i: i for i in range(kept)},
        compiler_params=params(),
        name=name,
    )(place, *ortho, *rights.values(), mine, other, *outs)


def per_device(grad, error, warm_right):
    dp = lax.axis_index("dp")
    core = dp & 1
    place = jnp.stack([dp >> 3, (dp >> 1) & 3, core]).astype(jnp.int32)

    other = half_of_memory(grad[0], error[0], (1 - core)[None])
    received = lax.ppermute(other, "dp", CORE)
    mine = half_of_memory(grad[0], error[0], core[None])
    pairs = pair_sum(place, mine, received)
    early, passed = early_left(place, warm_right.T, pairs)
    early = early + lax.ppermute(passed, "dp", CORE)
    early = stack_early(place, spread(early, "y", "y"))
    parts, early = lax.optimization_barrier((exchange(pairs, "z", "x"), early))
    rows = first_sum(place, parts)
    early = spread(early, "z", "x")
    parts, early = lax.optimization_barrier((exchange(rows, "x", "z"), early))
    piece = second_sum(place, parts)
    early = spread((early[0] + early[1]) + (early[2] + early[3]), "x", "z")
    m = jnp.concatenate(spread(piece, "x", "y"), axis=0)
    early = (early[0] + early[1]) + (early[2] + early[3])
    passed = lax.ppermute(early, "dp", CORE)
    m = spread(m, "y", "x")
    m, early, passed = lax.optimization_barrier((m, early, passed))

    left, own, oth = second_left(place, early, passed, m)
    own, oth, inverse = sum_over_group(own, oth, inverse_of(place, left))
    for step in range(ITERS - 2):
        left, own, oth = next_left(place, own, oth, inverse, m)
        own, oth, inverse = sum_over_group(own, oth, inverse_of(place, left))
    right, left, inverse = last_right(place, own, oth, inverse, m)

    near = {(0, 0): right, (0, 1): lax.ppermute(right, "dp", CORE)}
    *outs, ortho = finish(place, [left, inverse], near, mine, other, [], "finish_near")
    rights, outs = lax.optimization_barrier((spread(right, "z", "z"), outs))
    far = {(k, 0): rights[k] for k in (1, 2, 3)}
    far.update({(k, 1): lax.ppermute(rights[k], "dp", CORE) for k in (1, 2, 3)})
    update, new_error, right_t = finish(place, [ortho], far, mine, other, outs, "finish_far")
    return update, new_error[None], right_t.T


def solution(mesh):
    placed = (P("dp", "owner", None), P("dp", "owner", None), P())
    return jax.shard_map(
        per_device,
        mesh=mesh,
        in_specs=placed,
        out_specs=(P("owner", None), P("dp", "owner", None), P()),
        check_vma=False,
    )
```

```python
import jax
import jax.numpy as jnp
from jax import lax
from jax.experimental import pallas as pl
from jax.experimental.pallas import tpu as pltpu
from jax.sharding import PartitionSpec as P

W = 4096
RANK = 32
ITERS = 4
ROWS = 2048
N_DP = 32
N_OWNER = 4
HALF = W // 2
COLS = HALF // 4
ROWS_OWN = ROWS // N_OWNER
PIECE = ROWS_OWN // 4
MID = ROWS // 2
PANEL = 16
BF = jnp.bfloat16
F32 = jnp.float32
HIGHEST = lax.Precision.HIGHEST

CORE = [(i, i ^ 1) for i in range(N_DP)]
STEP = {"z": 32, "x": 8, "y": 1}


def along(array, first, second, k):
    step = (STEP[first], STEP[second])
    pairs = [(i, i ^ (k * step[(i >> 2) & 1])) for i in range(N_DP * N_OWNER)]
    return lax.ppermute(array, ("dp", "owner"), pairs)


def exchange(arrays, first, second):
    return [arrays[0]] + [along(arrays[k], first, second, k) for k in (1, 2, 3)]


def spread(array, first, second):
    return exchange([array] * 4, first, second)


def params(**kw):
    return pltpu.CompilerParams(vmem_limit_bytes=48 * 1024 * 1024, **kw)


SCALARS = pl.BlockSpec(memory_space=pltpu.SMEM)
WHOLE = pl.BlockSpec(memory_space=pltpu.VMEM)
HBM = pl.BlockSpec(memory_space=pl.ANY)
SMALL = pl.CostEstimate(flops=1000, bytes_accessed=1000, transcendentals=0)


def half_of_memory(grad, error, which):
    chunks = 8
    rows = ROWS_OWN // chunks

    def body(which_ref, g_hbm, e_hbm, o_ref, g_ref, e_ref, sems):
        cols = cut(which_ref[0], HALF)
        copies = []
        for i in range(chunks):
            part = pl.ds(i * rows, rows)
            pair = [
                pltpu.make_async_copy(src.at[part, cols], dst.at[part, :], sems.at[n, i])
                for n, (src, dst) in enumerate(((g_hbm, g_ref), (e_hbm, e_ref)))
            ]
            for copy in pair:
                copy.start()
            copies.append(pair)
        for i, pair in enumerate(copies):
            for copy in pair:
                copy.wait()
            part = pl.ds(i * rows, rows)
            o_ref[part, :] = (g_ref[part, :].astype(F32) + e_ref[part, :].astype(F32)).astype(BF)

    return pl.pallas_call(
        body,
        in_specs=[SCALARS, HBM, HBM],
        out_specs=WHOLE,
        scratch_shapes=[pltpu.VMEM((ROWS_OWN, HALF), BF)] * 2 + [pltpu.SemaphoreType.DMA((2, chunks))],
        out_shape=jax.ShapeDtypeStruct((ROWS_OWN, HALF), BF),
        compiler_params=params(),
        name="half_of_memory",
    )(which, grad, error)


def call(body, name, out_shape, place, *arrays, scratch=(), cost=None):
    return pl.pallas_call(
        body,
        in_specs=[SCALARS] + [WHOLE] * len(arrays),
        out_specs=jax.tree.map(lambda s: WHOLE, out_shape),
        out_shape=out_shape,
        scratch_shapes=scratch,
        cost_estimate=cost,
        compiler_params=params(),
        name=name,
    )(place, *arrays)


def cut(index, size):
    return pl.ds(pl.multiple_of(index * size, size), size)


def pair_sum(place, mine, received):
    def body(place_ref, a_ref, b_ref, *out):
        first = place_ref[2] == 0
        for k in range(4):
            for j in range(4):
                rows = cut(jnp.where(first, j, place_ref[1] ^ k), PIECE)
                cols = cut(jnp.where(first, place_ref[0] ^ k, j), COLS)
                out[k][j] = a_ref[rows, cols] + b_ref[rows, cols]

    return call(body, "pair_sum", [jax.ShapeDtypeStruct((4, PIECE, COLS), BF)] * 4, place, mine, received)


def first_sum(place, parts):
    def body(place_ref, *refs):
        own = jnp.where(place_ref[2] == 0, place_ref[1], place_ref[0])
        for k in range(4):
            total = refs[0][own ^ k].astype(F32)
            for ref in refs[1:4]:
                total = total + ref[own ^ k].astype(F32)
            refs[4 + k][...] = total.astype(BF)

    return call(body, "first_sum", [jax.ShapeDtypeStruct((PIECE, COLS), BF)] * 4, place, *parts)


def second_sum(place, parts):
    def body(place_ref, a_ref, b_ref, c_ref, d_ref, o_ref):
        total = a_ref[...].astype(F32) + b_ref[...].astype(F32)
        o_ref[...] = (total + (c_ref[...].astype(F32) + d_ref[...].astype(F32))).astype(BF)

    return call(body, "second_sum", jax.ShapeDtypeStruct((PIECE, COLS), BF), place, *parts)


def early_left(place, warm_t, pairs):
    def body(place_ref, warm_ref, *refs):
        pairs, (own_ref, oth_ref, sum_ref) = refs[:4], refs[4:]
        core = place_ref[2]
        sum_ref[...] = jnp.zeros((RANK, ROWS_OWN), F32)
        for k in range(4):
            for j in range(4):
                rows = cut(jnp.where(core == 0, j, place_ref[1] ^ k), PIECE)
                group = jnp.where(core == 0, place_ref[0] ^ k, j)
                right = warm_ref[:, cut(core * 4 + group, COLS)].astype(BF)
                sum_ref[:, rows] += dot(right, pairs[k][j], ((1,), (1,)))
        own_ref[...] = sum_ref[:, cut(core, ROWS_OWN // 2)]
        oth_ref[...] = sum_ref[:, cut(1 - core, ROWS_OWN // 2)]

    shapes = [jax.ShapeDtypeStruct((RANK, ROWS_OWN // 2), F32)] * 2
    scratch = [pltpu.VMEM((RANK, ROWS_OWN), F32)]
    return call(body, "early_left", shapes, place, warm_t, *pairs, scratch=scratch)


def stack_early(place, parts):
    def body(place_ref, a_ref, b_ref, c_ref, d_ref, o_ref):
        for i, ref in enumerate((a_ref, b_ref, c_ref, d_ref)):
            o_ref[i * RANK : (i + 1) * RANK, :] = ref[...]

    return call(body, "stack_early", jax.ShapeDtypeStruct((4 * RANK, ROWS_OWN // 2), F32), place, *parts)


def thirds(x):
    high = x.astype(BF)
    rest = x - high.astype(F32)
    mid = rest.astype(BF)
    low = (rest - mid.astype(F32)).astype(BF)
    return jnp.concatenate([high, mid, low], axis=0)


def dot(a, b, dims, precision=None):
    return lax.dot_general(a, b, ((dims[0], dims[1]), ((), ())), precision=precision, preferred_element_type=F32)


def thirds(x):
    high = x.astype(BF)
    rest = x - high.astype(F32)
    mid = rest.astype(BF)
    low = (rest - mid.astype(F32)).astype(BF)
    return jnp.concatenate([high, mid, low], axis=0)


def add_thirds(x):
    return x[:RANK] + (x[RANK : 2 * RANK] + x[2 * RANK :])


def reorder(rows, place_ref):
    blocks = [rows[:, i * PIECE : (i + 1) * PIECE] for i in range(16)]
    swapped = jnp.concatenate([blocks[(i % 4) * 4 + i // 4] for i in range(16)], axis=1)
    return jnp.where(place_ref[2] == 0, rows, swapped)


def store_halves(place_ref, left, own_ref, oth_ref):
    left = reorder(left, place_ref)
    low, high = left[:, :MID], left[:, MID:]
    first = place_ref[2] == 0
    own_ref[...] = jnp.where(first, low, high)
    oth_ref[...] = jnp.where(first, high, low)


def load_halves(place_ref, own_ref, oth_ref):
    first = place_ref[2] == 0
    own, oth = own_ref[...], oth_ref[...]
    return jnp.concatenate([jnp.where(first, own, oth), jnp.where(first, oth, own)], axis=1)


def times_m(rows, m_refs):
    parts = [dot(rows[:, i * ROWS_OWN : (i + 1) * ROWS_OWN], ref[...], ((1,), (0,))) for i, ref in enumerate(m_refs)]
    return (parts[0] + parts[1]) + (parts[2] + parts[3])


def times_m_t(rows, m_refs):
    return jnp.concatenate([dot(rows, ref[...], ((1,), (1,))) for ref in m_refs], axis=1)


def inverse_factor(gram):
    row = lax.broadcasted_iota(jnp.int32, (RANK, 128), 0)
    lane = lax.broadcasted_iota(jnp.int32, (RANK, 128), 1)
    wide = jnp.concatenate([gram, jnp.zeros((RANK, 128 - RANK), F32)], axis=1)
    trace = jnp.sum(jnp.where(row == lane, wide, 0.0), keepdims=True)
    shift = 1e-06 * (trace / RANK)
    work = wide + jnp.where(row == lane, shift, 0.0) + jnp.where(row + RANK == lane, 1.0, 0.0)
    for start in range(0, RANK, PANEL):
        cols = [jnp.broadcast_to(work[:, start + j : start + j + 1], (RANK, 128)) for j in range(PANEL)]
        for j in range(PANEL):
            k = start + j
            factor = jnp.where(row > k, cols[j] * (1.0 / cols[j][k : k + 1, :]), 0.0)
            work = work - factor * work[k : k + 1, :]
            for i in range(j + 1, PANEL):
                cols[i] = cols[i] - factor * cols[i][k : k + 1, :]
    pivot = jnp.sum(jnp.where(row == lane, work, 0.0), axis=1, keepdims=True)
    return work[:, RANK : 2 * RANK] * lax.rsqrt(pivot)


HALVES = [jax.ShapeDtypeStruct((RANK, MID), F32)] * 2


def from_left(place_ref, left, m_refs, own_ref, oth_ref):
    right = add_thirds(times_m(thirds(reorder(left, place_ref)), m_refs))
    store_halves(place_ref, add_thirds(times_m_t(thirds(right), m_refs)), own_ref, oth_ref)


def second_left(place, own, oth, m):
    def body(place_ref, own_in, oth_in, m0, m1, m2, m3, left_ref, own_ref, oth_ref, sum_ref):
        core, half = place_ref[2], ROWS_OWN // 2
        for y in range(4):
            rows = slice(y * RANK, (y + 1) * RANK)
            sum_ref[:, cut(2 * y + core, half)] = own_in[rows, :]
            sum_ref[:, cut(2 * y + 1 - core, half)] = oth_in[rows, :]
        for i in range(16):
            source = cut(i // 4 * 4 + (place_ref[1] ^ (i % 4)), PIECE)
            left_ref[:, i * PIECE : (i + 1) * PIECE] = sum_ref[:, source]
        from_left(place_ref, left_ref[...], (m0, m1, m2, m3), own_ref, oth_ref)

    shapes = [jax.ShapeDtypeStruct((RANK, ROWS), F32)] + HALVES
    return call(body, "second_left", shapes, place, own, oth, *m, scratch=[pltpu.VMEM((RANK, ROWS), F32)])


def next_left(place, own, oth, inverse, m):
    def body(place_ref, own_in, oth_in, inv_ref, m0, m1, m2, m3, left_ref, own_ref, oth_ref):
        left = load_halves(place_ref, own_in, oth_in)
        left = dot(inv_ref[...], left, ((1,), (0,)), HIGHEST) * (1.0 / N_DP)
        left_ref[...] = left
        from_left(place_ref, left, (m0, m1, m2, m3), own_ref, oth_ref)

    shapes = [jax.ShapeDtypeStruct((RANK, ROWS), F32)] + HALVES
    return call(body, "next_left", shapes, place, own, oth, inverse, *m)


def inverse_of(place, left):
    def body(place_ref, left_ref, o_ref):
        left = left_ref[...]
        o_ref[...] = inverse_factor(dot(left, left, ((1,), (1,)), HIGHEST))

    return call(body, "inverse_of", jax.ShapeDtypeStruct((RANK, RANK), F32), place, left, cost=SMALL)


def last_right(place, own, oth, inverse, m):
    def body(place_ref, own_in, oth_in, inv_ref, m0, m1, m2, m3, right_ref, left_ref, out_ref):
        left = load_halves(place_ref, own_in, oth_in)
        left = dot(inv_ref[...], left, ((1,), (0,)), HIGHEST) * (1.0 / N_DP)
        raw = add_thirds(times_m(thirds(reorder(left, place_ref)), (m0, m1, m2, m3)))
        inverse = inverse_factor(dot(left, left, ((1,), (1,)), HIGHEST))
        right_ref[...] = (dot(inverse, raw, ((1,), (0,)), HIGHEST) * (1.0 / N_DP)).astype(BF)
        for k in range(4):
            left_ref[:, cut(place_ref[1] ^ k, PIECE)] = left[:, k * PIECE : (k + 1) * PIECE]
        out_ref[...] = inverse

    shapes = [((RANK, COLS), BF), ((RANK, ROWS_OWN), F32), ((RANK, RANK), F32)]
    return call(body, "last_right", [jax.ShapeDtypeStruct(*s) for s in shapes], place, own, oth, inverse, *m)


def sum_over_group(own, oth, beside=None):
    own = own + lax.ppermute(oth, "dp", CORE)
    parts = spread(own, "z", "z")
    if beside is not None:
        parts, beside = lax.optimization_barrier((parts, beside))
    a, b, c, d = parts
    own = (a + b) + (c + d)
    return own, lax.ppermute(own, "dp", CORE), beside


def finish(place, ortho, rights, mine, other, outs, name):
    keys = list(rights)
    count, kept, made = len(keys), len(outs), len(ortho) == 2

    def body(place_ref, *refs):
        ortho_refs, refs = refs[: len(ortho)], refs[len(ortho) :]
        rights, memory, refs = refs[:count], refs[count : count + 2], refs[count + 2 + kept :]
        up_hbm, err_hbm, right_hbm = refs[:3]
        up_ref, err_ref, right_ref, sems = refs[-4:]
        o_ref = ortho_refs[0]
        if made:
            o_ref = refs[3]
            o_ref[...] = dot(ortho_refs[1][...], ortho_refs[0][...], ((1,), (0,)), HIGHEST).T.astype(BF)
        copies = []

        def send(i, n, source, target):
            copies.append(pltpu.make_async_copy(source, target, sems.at[i, n]))
            copies[-1].start()

        for n, ((k, j), ref) in enumerate(zip(keys, rights)):
            z = place_ref[0] ^ k
            cols = cut((place_ref[2] ^ j) * 4 + z, COLS)
            update = dot(o_ref[...], ref[...], ((1,), (0,)))
            up_ref[n] = update
            send(0, n, up_ref.at[n], up_hbm.at[:, cols])
            err_ref[n] = memory[j][:, cut(z, COLS)].astype(F32) - update
            send(1, n, err_ref.at[n], err_hbm.at[:, cols])
            right_ref[n] = ref[...].astype(F32)
            send(2, n, right_ref.at[n], right_hbm.at[:, cols])
        for copy in copies:
            copy.wait()

    blocks = pltpu.VMEM((count, ROWS_OWN, COLS), F32)
    return pl.pallas_call(
        body,
        in_specs=[SCALARS] + [WHOLE] * (len(ortho) + count + 2) + [HBM] * kept,
        out_specs=[HBM] * 3 + [WHOLE] * made,
        scratch_shapes=[blocks, blocks, pltpu.VMEM((count, RANK, COLS), F32), pltpu.SemaphoreType.DMA((3, count))],
        out_shape=(
            jax.ShapeDtypeStruct((ROWS_OWN, W), F32),
            jax.ShapeDtypeStruct((ROWS_OWN, W), F32),
            jax.ShapeDtypeStruct((RANK, W), F32),
        )
        + (jax.ShapeDtypeStruct((ROWS_OWN, RANK), BF),) * made,
        input_output_aliases={count + 4 + i: i for i in range(kept)},
        compiler_params=params(),
        name=name,
    )(place, *ortho, *rights.values(), mine, other, *outs)


def per_device(grad, error, warm_right):
    dp = lax.axis_index("dp")
    core = dp & 1
    place = jnp.stack([dp >> 3, (dp >> 1) & 3, core]).astype(jnp.int32)

    other = half_of_memory(grad[0], error[0], (1 - core)[None])
    received = lax.ppermute(other, "dp", CORE)
    mine = half_of_memory(grad[0], error[0], core[None])
    pairs = pair_sum(place, mine, received)
    early, passed = early_left(place, warm_right.T, pairs)
    early = early + lax.ppermute(passed, "dp", CORE)
    early = stack_early(place, spread(early, "y", "y"))
    parts, early = lax.optimization_barrier((exchange(pairs, "z", "x"), early))
    rows = first_sum(place, parts)
    early = spread(early, "x", "x")
    parts, early = lax.optimization_barrier((exchange(rows, "x", "z"), early))
    piece = second_sum(place, parts)
    early = spread((early[0] + early[1]) + (early[2] + early[3]), "z", "z")
    m = jnp.concatenate(spread(piece, "x", "y"), axis=0)
    early = (early[0] + early[1]) + (early[2] + early[3])
    passed = lax.ppermute(early, "dp", CORE)
    m = spread(m, "y", "x")
    m, early, passed = lax.optimization_barrier((m, early, passed))

    left, own, oth = second_left(place, early, passed, m)
    own, oth, inverse = sum_over_group(own, oth, inverse_of(place, left))
    for step in range(ITERS - 2):
        left, own, oth = next_left(place, own, oth, inverse, m)
        own, oth, inverse = sum_over_group(own, oth, inverse_of(place, left))
    right, left, inverse = last_right(place, own, oth, inverse, m)

    near = {(0, 0): right, (0, 1): lax.ppermute(right, "dp", CORE)}
    *outs, ortho = finish(place, [left, inverse], near, mine, other, [], "finish_near")
    rights, outs = lax.optimization_barrier((spread(right, "z", "z"), outs))
    far = {(k, 0): rights[k] for k in (1, 2, 3)}
    far.update({(k, 1): lax.ppermute(rights[k], "dp", CORE) for k in (1, 2, 3)})
    update, new_error, right_t = finish(place, [ortho], far, mine, other, outs, "finish_far")
    return update, new_error[None], right_t.T


def solution(mesh):
    placed = (P("dp", "owner", None), P("dp", "owner", None), P())
    return jax.shard_map(
        per_device,
        mesh=mesh,
        in_specs=placed,
        out_specs=(P("owner", None), P("dp", "owner", None), P()),
        check_vma=False,
    )
```
